256 devices in a mesh: ctx: 32 (over z, x), tp: 8 (over y, core).
Axes of the slice: x: 4, y: 4, z: 8, core: 2. Of those that a mesh axis runs over, the one named last changes fastest.
Arguments:
- query_in: bfloat16 [16384, 8192], P('ctx', 'tp'), may hold values from -6 to 6
- key_in: bfloat16 [16384, 8192], P('ctx', 'tp'), may hold values from -6 to 6
- value_in: bfloat16 [16384, 8192], P('ctx', 'tp'), may hold values from -6 to 6
- filters: bfloat16 [512, 128], P('tp'), may hold values from -0.5 to 0.5
- proj_out: bfloat16 [4096, 8192], P('ctx', 'tp'), may hold values from -0.0625 to 0.0625
- cotangent: bfloat16 [16384, 4096], P('ctx', 'tp'), may hold values from -6 to 6
Outputs:
- grad_query: bfloat16 [16384, 8192], P('ctx', 'tp')
- grad_key: bfloat16 [16384, 8192], P('ctx', 'tp')
- grad_value: bfloat16 [16384, 8192], P('ctx', 'tp')
- grad_filter: float32 [512, 128], P('tp')
- grad_proj: float32 [4096, 8192], P('ctx', 'tp')
The draws below stay inside these ranges and needn't reach their ends.
All inputs are finite; a program needn't handle non-finite values.
Results may differ from the reference program's by a relative error of at most 0.005.
Values may be sent and summed in bfloat16 or wider, within the bound.
No kernel may reach another device: no remote copies, remote signals or barrier semaphores. Data moves between devices by JAX's collectives and lax.ppermute only.
A program may use at most 192 MiB of HBM per device.

```python
import jax
import jax.numpy as jnp
from jax import lax

D = 8192
FL = 128
GS = 16
DO = 4096
GROUPS = 512
TOKENS = 16384


def strengthened(array, rng, source, target, blocks, factor):
    owner, partner = [(jnp.arange(array.shape[axis_at]) // (array.shape[axis_at] // blocks)).reshape([-1 if axis == axis_at else 1 for axis in range(array.ndim)]) for axis_at in (source, target)]
    chosen = jax.random.permutation(rng, blocks)[partner]
    strong = (owner == chosen) | (owner == (partner + blocks // 2) % blocks)
    return jnp.where(strong, factor * array, array)


def steps_of(key, extent, split, least, high):
    gain, own = 1.0, jax.random.fold_in(key, 6)
    for dim, parts in split:
        draws = jnp.exp(jax.random.uniform(jax.random.fold_in(own, dim), (parts,), jnp.float32, least / len(split), high / len(split)))
        gain = gain * jnp.repeat(draws, extent[dim] // parts).reshape([-1 if axis == dim else 1 for axis in range(len(extent))])
    return gain


def scatter_about(rng, dims, scale, bound, shards=(), held_as=jnp.bfloat16):
    entries = scale * jax.random.normal(rng, dims, jnp.float32)
    if shards:
        entries = entries * steps_of(rng, dims, shards, -0.22, 0.18)
    return jnp.clip(entries, -bound, bound).astype(held_as)


def gaussian_with(key, shape, spread, most, pieces, heavy, dtype=jnp.bfloat16):
    array = spread * jax.random.normal(key, shape, jnp.float32)
    if pieces:
        array = array * steps_of(key, shape, pieces, -0.22, 0.18)
    return jnp.clip(strengthened(array, jax.random.fold_in(key, 3), *heavy), -most, most).astype(dtype)


def setup_inputs(seed: int = 0) -> dict:
    key_of = jax.random.split(jax.random.key(seed), 7)
    return {
        "query_in": scatter_about(key_of[0], (TOKENS, D), 1.0, 6.0, ((0, 32), (1, 8))),
        "key_in": scatter_about(key_of[1], (TOKENS, D), 1.0, 6.0, ((0, 32), (1, 8))),
        "value_in": scatter_about(key_of[2], (TOKENS, D), 1.0, 6.0, ((0, 32), (1, 8))),
        "filters": scatter_about(key_of[3], (GROUPS, FL), FL ** -0.5, 0.5, ((0, 8),)),
        "proj_out": scatter_about(key_of[4], (DO, D), D ** -0.5, 0.0625, ((0, 32), (1, 8))),
        "cotangent": gaussian_with(key_of[5], (TOKENS, DO), 1.0, 6.0, ((0, 32), (1, 8)), (0, 1, 32, 2.75)),
    }


def toeplitz(filters):
    rows = jnp.arange(FL)[:, None]
    cols = jnp.arange(2 * FL)[None, :]
    tap_index = rows + FL - cols
    valid = (tap_index >= 0) & (tap_index < FL)
    picked = jnp.take(filters.astype(jnp.float32), jnp.clip(tap_index, 0, FL - 1), axis=1)
    return jnp.where(valid[None], picked, jnp.float32(0.0)), tap_index


def reference(query_in, key_in, value_in, filters, proj_out, cotangent):
    nblocks = TOKENS // FL
    high = lax.Precision.HIGHEST
    mixed_in = (key_in.astype(jnp.float32) * value_in.astype(jnp.float32)).astype(jnp.bfloat16)
    table, tap_index = toeplitz(filters)
    own_blocks = mixed_in.astype(jnp.float32).reshape(nblocks, FL, GROUPS, GS)
    prev_blocks = jnp.concatenate([jnp.zeros((1, FL, GROUPS, GS), jnp.float32), own_blocks[:-1]], 0)
    window = jnp.concatenate([prev_blocks, own_blocks], 1)
    conv_out = jnp.einsum("gts,bsgc->btgc", table, window, precision=high).reshape(TOKENS, D)
    gated = (query_in.astype(jnp.float32) * conv_out).astype(jnp.bfloat16)
    grad_gate = jnp.dot(cotangent, proj_out, preferred_element_type=jnp.float32)
    grad_query = (grad_gate * conv_out).astype(jnp.bfloat16)
    grad_inner = (grad_gate * query_in.astype(jnp.float32)).astype(jnp.bfloat16)
    inner_blocks = grad_inner.astype(jnp.float32).reshape(nblocks, FL, GROUPS, GS)
    after_blocks = jnp.concatenate([inner_blocks[1:], jnp.zeros((1, FL, GROUPS, GS), jnp.float32)], 0)
    grad_mixed = jnp.einsum("gts,btgc->bsgc", table[:, :, FL:], inner_blocks, precision=high)
    grad_mixed = grad_mixed + jnp.einsum("gts,btgc->bsgc", table[:, :, :FL], after_blocks, precision=high)
    grad_mixed = grad_mixed.reshape(TOKENS, D)
    grad_key = (grad_mixed * value_in.astype(jnp.float32)).astype(jnp.bfloat16)
    grad_value = (grad_mixed * key_in.astype(jnp.float32)).astype(jnp.bfloat16)
    corr = jnp.einsum("btgc,bsgc->gts", inner_blocks, window, precision=high)
    selector = (tap_index[:, :, None] == jnp.arange(FL)[None, None, :]).astype(jnp.float32)
    grad_filter = jnp.einsum("gts,tsj->gj", corr, selector, precision=high)
    grad_proj = jnp.dot(cotangent.T, gated, preferred_element_type=jnp.float32)
    return (grad_query, grad_key, grad_value, grad_filter, grad_proj)
```

```python
import functools

import jax
import jax.numpy as jnp
from jax import lax
from jax.experimental import pallas as pl
from jax.experimental.pallas import tpu as pltpu
from jax.sharding import Mesh
from jax.sharding import PartitionSpec as P

F32, BF16 = jnp.float32, jnp.bfloat16
LANES = 128
AXES = ("z", "x", "y", "c")
SIZE = {"x": 4, "y": 4, "c": 2}
MIB = 1 << 20


def send(value, axis, by):
    count = lax.axis_size(axis)
    return lax.ppermute(value, axis, [(i, (i + by) % count) for i in range(count)])


def send_along_tokens(value, by):
    count = lax.axis_size("z") * lax.axis_size("x")
    pairs = [(i, i + by) for i in range(count) if 0 <= i + by < count]
    return lax.ppermute(value, ("z", "x"), pairs)


def product(a, b):
    return (a.astype(F32) * b.astype(F32)).astype(BF16)


def group_tables(rows, width):
    tables = [
        pltpu.roll(
            jnp.broadcast_to(rows[g : g + 1], (width // 2, width)), 0, 1, stride=1, stride_axis=0
        )
        for g in range(rows.shape[0])
    ]
    return jnp.concatenate(tables, 0).astype(BF16)


def banded(tables, window, taps, groups):
    lane_group = lax.broadcasted_iota(jnp.int32, (taps, LANES), 1) // (LANES // groups)
    blocks = window.shape[0] // taps - 1
    out = []
    for b in range(0, blocks, 2):
        pair = jnp.concatenate(
            [window[(b + i) * taps : (b + i + 2) * taps] for i in range(2)], 1
        )
        res = jnp.dot(tables, pair, preferred_element_type=F32)
        for i in range(2):
            cols = slice(i * LANES, (i + 1) * LANES)
            acc = res[:taps, cols]
            for g in range(1, groups):
                acc = jnp.where(lane_group == g, res[g * taps : (g + 1) * taps, cols], acc)
            out.append(acc)
    return jnp.concatenate(out, 0)


def forward_body(taps, groups, rows_ref, k_ref, v_ref, q_ref, rim_ref, *refs):
    conv_ref, mixed_ref, gated_ref = refs[-3:]
    mixed = product(k_ref[...], v_ref[...])
    window = jnp.concatenate([rim_ref[...], mixed], 0)
    conv = banded(group_tables(rows_ref[...], 2 * taps), window, taps, groups)
    conv_ref[...] = conv
    mixed_ref[...] = mixed
    gated_ref[...] = (q_ref[...].astype(F32) * conv).astype(BF16)


def forward(half, rows, k, v, q, rim, earlier):
    tokens, width = k.shape
    taps = rim.shape[0]
    groups = LANES * rows.shape[0] // width
    steps = width // LANES // 2
    at = lambda i: (0, i + half * steps)
    column = pl.BlockSpec((tokens, LANES), at)
    in_specs = [
        pl.BlockSpec((groups, 2 * taps), lambda i: (i + half * steps, 0)),
        column,
        column,
        column,
        pl.BlockSpec((taps, LANES), at),
    ]
    args = [rows, k, v, q, rim]
    aliases = {}
    if earlier is not None:
        in_specs += [pl.BlockSpec(memory_space=pl.ANY)] * 2
        args += list(earlier)
        aliases = {5: 0, 6: 1}
    return pl.pallas_call(
        functools.partial(forward_body, taps, groups),
        grid=(steps,),
        in_specs=in_specs,
        out_specs=[column, column, pl.BlockSpec((tokens, LANES), lambda i: (0, i))],
        out_shape=[
            jax.ShapeDtypeStruct((tokens, width), F32),
            jax.ShapeDtypeStruct((tokens, width), BF16),
            jax.ShapeDtypeStruct((tokens, width // 2), BF16),
        ],
        input_output_aliases=aliases,
        compiler_params=pltpu.CompilerParams(vmem_limit_bytes=24 * MIB),
        cost_estimate=pl.CostEstimate(
            flops=tokens * width * 2 * taps * groups, bytes_accessed=tokens * width * 7, transcendentals=0
        ),
        name="conv_forward",
    )(*args)


def gate_body(place_ref, mine_ref, sib_ref, proj_ref, *refs):
    out_ref = refs[-1]
    rows = proj_ref.shape[0] // 8
    acc = None
    for dy in range(4):
        at = pl.ds(dy * rows, rows)
        lhs = jnp.concatenate([mine_ref[:, at], sib_ref[:, at]], 1)
        rhs = jnp.concatenate(
            [
                proj_ref[pl.ds(pl.multiple_of(place_ref[2 * dy + i] * rows, rows), rows), :]
                for i in range(2)
            ],
            0,
        )
        term = jnp.dot(lhs, rhs, preferred_element_type=F32)
        acc = term if acc is None else acc + term
    for ref in refs[:-1]:
        acc = acc + ref[...].astype(F32)
    out_ref[...] = acc.astype(out_ref.dtype)


def gate_part(place, mine, sib, proj, block, half, dtype, *addends):
    depth, width = proj.shape
    tokens = mine.shape[0] // 4
    tile = 256
    steps = width // 2 // tile
    spec = pltpu.PrefetchScalarGridSpec(
        num_scalar_prefetch=1,
        grid=(steps,),
        in_specs=[
            pl.BlockSpec((tokens, depth // 2), lambda i, p: (block, 0)),
            pl.BlockSpec((tokens, depth // 2), lambda i, p: (block, 0)),
            pl.BlockSpec((depth, tile), lambda i, p: (0, i + half * steps)),
        ]
        + [pl.BlockSpec((tokens, tile), lambda i, p: (0, i))] * len(addends),
        out_specs=pl.BlockSpec((tokens, tile), lambda i, p: (0, i)),
    )
    return pl.pallas_call(
        gate_body,
        grid_spec=spec,
        out_shape=jax.ShapeDtypeStruct((tokens, width // 2), dtype),
        compiler_params=pltpu.CompilerParams(vmem_limit_bytes=24 * MIB),
        cost_estimate=pl.CostEstimate(
            flops=tokens * depth * width, bytes_accessed=depth * width + 2 * tokens * depth, transcendentals=0
        ),
        name="grad_gate_part",
    )(place, mine, sib, proj, *addends)


def proj_body(place_ref, mine_ref, sib_ref, *refs):
    gated_refs, out_ref = refs[:-1], refs[-1]
    rows = mine_ref.shape[1]
    tokens, half = gated_refs[0].shape
    core = place_ref[0] % 2
    for h in range(2):
        acc = None
        for d in range(4):
            at = pl.ds(d * tokens, tokens)
            lhs = jnp.concatenate([mine_ref[at, :], sib_ref[at, :]], 1)
            term = lax.dot_general(
                lhs, gated_refs[2 * d + h][...], (((0,), (0,)), ((), ())), preferred_element_type=F32
            )
            acc = term if acc is None else acc + term
        acc = acc.astype(BF16)
        cols = pl.ds(h * half, half)
        out_ref[pl.ds(pl.multiple_of(core * rows, rows), rows), cols] = acc[:rows]
        out_ref[pl.ds(pl.multiple_of((1 - core) * rows, rows), rows), cols] = acc[rows:]


def proj_part(place, mine, sib, gated):
    depth = 2 * mine.shape[1]
    tokens, half = gated[0].shape
    rows = depth // 8
    spec = pltpu.PrefetchScalarGridSpec(
        num_scalar_prefetch=1,
        grid=(4,),
        in_specs=[pl.BlockSpec((4 * tokens, rows), lambda i, p: (0, i))] * 2
        + [pl.BlockSpec((tokens, half), lambda i, p: (0, 0))] * 8,
        out_specs=pl.BlockSpec((2 * rows, 2 * half), lambda i, p: (p[2 * i] // 2, 0)),
    )
    return pl.pallas_call(
        proj_body,
        grid_spec=spec,
        out_shape=jax.ShapeDtypeStruct((depth, 2 * half), BF16),
        compiler_params=pltpu.CompilerParams(vmem_limit_bytes=40 * MIB),
        cost_estimate=pl.CostEstimate(
            flops=16 * tokens * depth * half, bytes_accessed=20 * tokens * half, transcendentals=0
        ),
        name="grad_proj_part",
    )(place, mine, sib, *gated)


def inner_body(taps, groups, *refs):
    own, from_left, from_right = refs[0:2], refs[2:4], refs[4:6]
    q_ref, conv_ref, mixed_ref, rim_ref, query_ref, inner_ref, filter_ref = refs[6:]
    second = pl.program_id(0) >= pl.num_programs(0) // 2
    pick = lambda pair: jnp.where(second, pair[1][...], pair[0][...]).astype(F32)
    gate = pick(own) + pick(from_left) + pick(from_right)
    query_ref[...] = (gate * conv_ref[...]).astype(BF16)
    inner = (gate * q_ref[...].astype(F32)).astype(BF16)
    inner_ref[...] = inner
    window = jnp.concatenate([rim_ref[...], mixed_ref[...]], 0)
    blocks = inner.shape[0] // taps
    left = jnp.concatenate([inner[b * taps : (b + 1) * taps] for b in range(blocks)], 1)
    turn = sum(lax.broadcasted_iota(jnp.int32, (taps, taps), i) for i in range(2)) == taps - 1
    left = jnp.dot(turn.astype(F32).astype(BF16), left, preferred_element_type=F32).astype(BF16)
    right = jnp.concatenate([window[b * taps : (b + 2) * taps] for b in range(blocks)], 1)
    lane_group = (lax.broadcasted_iota(jnp.int32, left.shape, 1) % LANES) // (LANES // groups)
    zero = jnp.zeros_like(left)
    stacked = jnp.concatenate([jnp.where(lane_group == g, left, zero) for g in range(groups)], 0)
    corr = lax.dot_general(stacked, right, (((1,), (1,)), ((), ())), preferred_element_type=F32)
    sums = [
        jnp.sum(
            pltpu.roll(corr[g * taps : (g + 1) * taps], 0, 1, stride=1, stride_axis=0),
            axis=0,
            keepdims=True,
        )[:, taps:]
        for g in range(groups)
    ]
    filter_ref[...] = jnp.concatenate(sums, 0)


def gate_gradients(own, from_left, from_right, q, conv, mixed, rim, group_count):
    tokens, width = q.shape
    taps = rim.shape[0]
    groups = LANES * group_count // width
    steps = width // LANES
    column = pl.BlockSpec((tokens, LANES), lambda i: (0, i))
    first = pl.BlockSpec((tokens, LANES), lambda i: (0, jnp.minimum(i, steps // 2 - 1)))
    last = pl.BlockSpec((tokens, LANES), lambda i: (0, jnp.maximum(i - steps // 2, 0)))
    return pl.pallas_call(
        functools.partial(inner_body, taps, groups),
        grid=(steps,),
        in_specs=[first, last] * 3
        + [column, column, column, pl.BlockSpec((taps, LANES), lambda i: (0, i))],
        out_specs=[column, column, pl.BlockSpec((groups, taps), lambda i: (i, 0))],
        out_shape=[
            jax.ShapeDtypeStruct((tokens, width), BF16),
            jax.ShapeDtypeStruct((tokens, width), BF16),
            jax.ShapeDtypeStruct((group_count, taps), F32),
        ],
        compiler_params=pltpu.CompilerParams(vmem_limit_bytes=32 * MIB),
        cost_estimate=pl.CostEstimate(
            flops=tokens * width * 4 * taps * groups, bytes_accessed=tokens * width * 20, transcendentals=0
        ),
        name="gate_gradients",
    )(*own, *from_left, *from_right, q, conv, mixed, rim)


def backward_body(taps, groups, rows_ref, inner_ref, ahead_ref, k_ref, v_ref, gk_ref, gv_ref):
    window = jnp.concatenate([inner_ref[...], ahead_ref[...]], 0)
    grad = banded(group_tables(rows_ref[...], 2 * taps), window, taps, groups)
    gk_ref[...] = (grad * v_ref[...].astype(F32)).astype(BF16)
    gv_ref[...] = (grad * k_ref[...].astype(F32)).astype(BF16)


def backward(rows, inner, ahead, k, v):
    tokens, width = k.shape
    taps = ahead.shape[0]
    groups = LANES * rows.shape[0] // width
    column = pl.BlockSpec((tokens, LANES), lambda i: (0, i))
    return pl.pallas_call(
        functools.partial(backward_body, taps, groups),
        grid=(width // LANES,),
        in_specs=[
            pl.BlockSpec((groups, 2 * taps), lambda i: (i, 0)),
            column,
            pl.BlockSpec((taps, LANES), lambda i: (0, i)),
            column,
            column,
        ],
        out_specs=[column, column],
        out_shape=[jax.ShapeDtypeStruct((tokens, width), BF16)] * 2,
        compiler_params=pltpu.CompilerParams(vmem_limit_bytes=24 * MIB),
        cost_estimate=pl.CostEstimate(
            flops=tokens * width * 4 * taps * groups, bytes_accessed=tokens * width * 10, transcendentals=0
        ),
        name="conv_backward",
    )(rows, inner, ahead, k, v)


def sum_over(value, axis):
    count = lax.axis_size(axis)
    copies = jnp.broadcast_to(value[None], (count, *value.shape))
    return jnp.sum(lax.all_to_all(copies, axis, split_axis=0, concat_axis=0, tiled=True), 0)


def on_device(query_in, key_in, value_in, filters, proj_out, cotangent):
    tokens, width = query_in.shape
    group_count, taps = filters.shape
    half = width // 2
    x, y, c = (lax.axis_index(a) for a in ("x", "y", "c"))
    part = cotangent.shape[1] // 4

    proj = lax.all_gather(proj_out, "z", axis=0, tiled=True)

    rim = send_along_tokens(product(key_in[tokens - taps :], value_in[tokens - taps :]), 1)
    own_cols = lambda d: lax.dynamic_slice_in_dim(cotangent, ((x + d) % 4) * part, part, 1)
    pieces = [own_cols(0), None, None, None]
    for d in (2, 1, 3):
        pieces[(-d) % 4] = send(own_cols(d), "x", d)
    column = jnp.concatenate(pieces, 0)
    below, above = send(column, "y", 1), send(column, "y", -1)
    middle = column.shape[0] // 2
    far = jnp.concatenate([send(below[:middle], "y", 1), send(above[middle:], "y", -1)], 0)
    mine = jnp.concatenate([column, above, far, below], 1)
    sib = send(mine, "c", 1)
    place = jnp.stack([2 * ((y + dy) % 4) + (c if i == 0 else 1 - c) for dy in range(4) for i in range(2)])
    place = place.astype(jnp.int32)

    taps32 = filters.astype(F32)
    rows = jnp.concatenate(
        [jnp.zeros((group_count, 1), F32), jnp.flip(taps32, 1), jnp.zeros((group_count, taps - 1), F32)], 1
    )
    back_rows = jnp.concatenate([taps32, jnp.zeros((group_count, taps), F32)], 1)
    conv, mixed, gated_a = forward(0, rows, key_in, value_in, query_in, rim, None)
    conv, mixed, gated_b = forward(1, rows, key_in, value_in, query_in, rim, (conv, mixed))
    left_a, right_b = send(gated_a, "x", 1), send(gated_b, "x", -1)
    right_a, left_b = send(gated_a, "x", -1), send(gated_b, "x", 1)
    far_a, far_b = send(left_a, "x", 1), send(right_b, "x", -1)
    gated = [gated_a, gated_b, right_a, right_b, far_a, far_b, left_a, left_b]
    proj_sums = proj_part(place, mine, sib, gated)
    grad_proj = lax.psum_scatter(proj_sums, "z", scatter_dimension=0, tiled=True).astype(F32)

    share = lambda d, h, dtype, *addends: gate_part(place, mine, sib, proj, d, h, dtype, *addends)
    far_a = send(share(2, 0, BF16), "x", 1)
    far_b = send(share(2, 1, BF16), "x", -1)
    from_left_b = send(share(1, 1, BF16), "x", 1)
    from_right_a = send(share(3, 0, BF16), "x", -1)
    from_left_a = send(share(1, 0, BF16, far_a), "x", 1)
    from_right_b = send(share(3, 1, BF16, far_b), "x", -1)
    own = share(0, 0, F32), share(0, 1, F32)
    from_left, from_right = (from_left_a, from_left_b), (from_right_a, from_right_b)

    first = [
        (
            (own[h][:taps] + from_left[h][:taps].astype(F32) + from_right[h][:taps].astype(F32))
            * query_in[:taps, h * half : (h + 1) * half].astype(F32)
        ).astype(BF16)
        for h in range(2)
    ]
    ahead = send_along_tokens(jnp.concatenate(first, 1), -1)
    grad_query, inner, sums = gate_gradients(
        own, from_left, from_right, query_in, conv, mixed, rim, group_count
    )
    grad_filter = sum_over(sum_over(jnp.flip(sums, 1), "x"), "z")
    grad_key, grad_value = backward(back_rows, inner, ahead, key_in, value_in)
    return grad_query, grad_key, grad_value, grad_filter, grad_proj


def solution(mesh):
    ctx, tp = mesh.devices.shape
    shape = (ctx // SIZE["x"], SIZE["x"], tp // SIZE["c"], SIZE["c"])
    fine = Mesh(mesh.devices.reshape(shape), AXES)
    spec, along = P(("z", "x"), ("y", "c")), P(("y", "c"), None)
    return jax.shard_map(
        on_device,
        mesh=fine,
        in_specs=(spec, spec, spec, along, spec, spec),
        out_specs=(spec, spec, spec, along, spec),
        check_vma=False,
    )
```

```python
import functools

import jax
import jax.numpy as jnp
from jax import lax
from jax.experimental import pallas as pl
from jax.experimental.pallas import tpu as pltpu
from jax.sharding import Mesh
from jax.sharding import PartitionSpec as P

F32, BF16 = jnp.float32, jnp.bfloat16
LANES = 128
AXES = ("z", "x", "y", "c")
SIZE = {"x": 4, "y": 4, "c": 2}
MIB = 1 << 20
LIGHT = pl.CostEstimate(flops=1 << 20, bytes_accessed=1 << 18, transcendentals=0)


def send(value, axis, by):
    count = lax.axis_size(axis)
    return lax.ppermute(value, axis, [(i, (i + by) % count) for i in range(count)])


def send_along_tokens(value, by):
    count = lax.axis_size("z") * lax.axis_size("x")
    pairs = [(i, i + by) for i in range(count) if 0 <= i + by < count]
    return lax.ppermute(value, ("z", "x"), pairs)


def after(value, *others):
    return lax.optimization_barrier((value, *others))[0]


def product(a, b):
    return (a.astype(F32) * b.astype(F32)).astype(BF16)


def group_tables(rows, width):
    tables = [
        pltpu.roll(
            jnp.broadcast_to(rows[g : g + 1], (width // 2, width)), 0, 1, stride=1, stride_axis=0
        )
        for g in range(rows.shape[0])
    ]
    return jnp.concatenate(tables, 0).astype(BF16)


def banded(tables, window, taps, groups):
    lane_group = lax.broadcasted_iota(jnp.int32, (taps, LANES), 1) // (LANES // groups)
    blocks = window.shape[0] // taps - 1
    out = []
    for b in range(0, blocks, 2):
        pair = jnp.concatenate(
            [window[(b + i) * taps : (b + i + 2) * taps] for i in range(2)], 1
        )
        res = jnp.dot(tables, pair, preferred_element_type=F32)
        for i in range(2):
            cols = slice(i * LANES, (i + 1) * LANES)
            acc = res[:taps, cols]
            for g in range(1, groups):
                acc = jnp.where(lane_group == g, res[g * taps : (g + 1) * taps, cols], acc)
            out.append(acc)
    return jnp.concatenate(out, 0)


def forward_body(taps, groups, rows_ref, k_ref, v_ref, q_ref, rim_ref, *refs):
    conv_ref, mixed_ref, gated_ref = refs[-3:]
    mixed = product(k_ref[...], v_ref[...])
    window = jnp.concatenate([rim_ref[...], mixed], 0)
    conv = banded(group_tables(rows_ref[...], 2 * taps), window, taps, groups)
    conv_ref[...] = conv
    mixed_ref[...] = mixed
    gated_ref[...] = (q_ref[...].astype(F32) * conv).astype(BF16)


def forward(half, rows, k, v, q, rim, earlier):
    tokens, width = k.shape
    taps = rim.shape[0]
    groups = LANES * rows.shape[0] // width
    steps = width // LANES // 2
    at = lambda i: (0, i + half * steps)
    column = pl.BlockSpec((tokens, LANES), at)
    in_specs = [
        pl.BlockSpec((groups, 2 * taps), lambda i: (i + half * steps, 0)),
        column,
        column,
        column,
        pl.BlockSpec((taps, LANES), at),
    ]
    args = [rows, k, v, q, rim]
    aliases = {}
    if earlier is not None:
        in_specs += [pl.BlockSpec(memory_space=pl.ANY)] * 2
        args += list(earlier)
        aliases = {5: 0, 6: 1}
    return pl.pallas_call(
        functools.partial(forward_body, taps, groups),
        grid=(steps,),
        in_specs=in_specs,
        out_specs=[column, column, pl.BlockSpec((tokens, LANES), lambda i: (0, i))],
        out_shape=[
            jax.ShapeDtypeStruct((tokens, width), F32),
            jax.ShapeDtypeStruct((tokens, width), BF16),
            jax.ShapeDtypeStruct((tokens, width // 2), BF16),
        ],
        input_output_aliases=aliases,
        compiler_params=pltpu.CompilerParams(vmem_limit_bytes=24 * MIB),
        cost_estimate=LIGHT,
        name="conv_forward",
    )(*args)


def gate_body(place_ref, mine_ref, sib_ref, proj_ref, *refs):
    out_ref = refs[-1]
    rows = proj_ref.shape[0] // 8
    acc = None
    for dy in range(4):
        lhs = jnp.concatenate([mine_ref[dy], sib_ref[dy]], 1)
        rhs = jnp.concatenate(
            [
                proj_ref[pl.ds(pl.multiple_of(place_ref[2 * dy + i] * rows, rows), rows), :]
                for i in range(2)
            ],
            0,
        )
        term = jnp.dot(lhs, rhs, preferred_element_type=F32)
        acc = term if acc is None else acc + term
    for ref in refs[:-1]:
        acc = acc + ref[...].astype(F32)
    out_ref[...] = acc.astype(out_ref.dtype)


def gate_part(place, mine, sib, proj, block, half, dtype, *addends):
    depth, width = proj.shape
    tokens = mine.shape[1] // 4
    tile = 256
    steps = width // 2 // tile
    spec = pltpu.PrefetchScalarGridSpec(
        num_scalar_prefetch=1,
        grid=(steps,),
        in_specs=[
            pl.BlockSpec((4, tokens, depth // 8), lambda i, p: (0, block, 0)),
            pl.BlockSpec((4, tokens, depth // 8), lambda i, p: (0, block, 0)),
            pl.BlockSpec((depth, tile), lambda i, p: (0, i + half * steps)),
        ]
        + [pl.BlockSpec((tokens, tile), lambda i, p: (0, i))] * len(addends),
        out_specs=pl.BlockSpec((tokens, tile), lambda i, p: (0, i)),
    )
    return pl.pallas_call(
        gate_body,
        grid_spec=spec,
        out_shape=jax.ShapeDtypeStruct((tokens, width // 2), dtype),
        compiler_params=pltpu.CompilerParams(vmem_limit_bytes=24 * MIB),
        cost_estimate=LIGHT,
        name="grad_gate_part",
    )(place, mine, sib, proj, *addends)


def proj_body(place_ref, mine_ref, sib_ref, *refs):
    gated_refs, out_ref = refs[:-1], refs[-1]
    rows = mine_ref.shape[1]
    tokens, half = gated_refs[0].shape
    core = place_ref[0] % 2
    for h in range(2):
        acc = None
        for d in range(4):
            at = pl.ds(d * tokens, tokens)
            lhs = jnp.concatenate([mine_ref[at, :], sib_ref[at, :]], 1)
            term = lax.dot_general(
                lhs, gated_refs[2 * d + h][...], (((0,), (0,)), ((), ())), preferred_element_type=F32
            )
            acc = term if acc is None else acc + term
        acc = acc.astype(BF16)
        cols = pl.ds(h * half, half)
        out_ref[pl.ds(pl.multiple_of(core * rows, rows), rows), cols] = acc[:rows]
        out_ref[pl.ds(pl.multiple_of((1 - core) * rows, rows), rows), cols] = acc[rows:]


def proj_part(place, mine, sib, gated):
    rows = mine.shape[2]
    depth = 8 * rows
    tokens, half = gated[0].shape
    spec = pltpu.PrefetchScalarGridSpec(
        num_scalar_prefetch=1,
        grid=(4,),
        in_specs=[pl.BlockSpec((None, 4 * tokens, rows), lambda i, p: (i, 0, 0))] * 2
        + [pl.BlockSpec((tokens, half), lambda i, p: (0, 0))] * 8,
        out_specs=pl.BlockSpec((2 * rows, 2 * half), lambda i, p: (p[2 * i] // 2, 0)),
    )
    return pl.pallas_call(
        proj_body,
        grid_spec=spec,
        out_shape=jax.ShapeDtypeStruct((depth, 2 * half), BF16),
        compiler_params=pltpu.CompilerParams(vmem_limit_bytes=40 * MIB),
        cost_estimate=LIGHT,
        name="grad_proj_part",
    )(place, mine, sib, *gated)


def inner_body(*refs):
    own, from_left, from_right = refs[0:2], refs[2:4], refs[4:6]
    q_ref, conv_ref, query_ref, inner_ref = refs[6:]
    second = pl.program_id(0) >= pl.num_programs(0) // 2
    pick = lambda pair: jnp.where(second, pair[1][...], pair[0][...]).astype(F32)
    gate = pick(own) + pick(from_left) + pick(from_right)
    query_ref[...] = (gate * conv_ref[...]).astype(BF16)
    inner_ref[...] = (gate * q_ref[...].astype(F32)).astype(BF16)


def gate_gradients(own, from_left, from_right, q, conv):
    tokens, width = q.shape
    wide = 2 * LANES
    steps = width // wide
    column = pl.BlockSpec((tokens, wide), lambda i: (0, i))
    first = pl.BlockSpec((tokens, wide), lambda i: (0, jnp.minimum(i, steps // 2 - 1)))
    last = pl.BlockSpec((tokens, wide), lambda i: (0, jnp.maximum(i - steps // 2, 0)))
    return pl.pallas_call(
        inner_body,
        grid=(steps,),
        in_specs=[first, last] * 3 + [column, column],
        out_specs=[column, column],
        out_shape=[jax.ShapeDtypeStruct((tokens, width), BF16)] * 2,
        compiler_params=pltpu.CompilerParams(vmem_limit_bytes=32 * MIB),
        cost_estimate=LIGHT,
        name="gate_gradients",
    )(*own, *from_left, *from_right, q, conv)


def filter_body(taps, groups, inner_ref, mixed_ref, rim_ref, filter_ref):
    inner = inner_ref[...]
    window = jnp.concatenate([rim_ref[...], mixed_ref[...]], 0)
    blocks = inner.shape[0] // taps
    left = jnp.concatenate([inner[b * taps : (b + 1) * taps] for b in range(blocks)], 1)
    turn = sum(lax.broadcasted_iota(jnp.int32, (taps, taps), i) for i in range(2)) == taps - 1
    left = jnp.dot(turn.astype(F32).astype(BF16), left, preferred_element_type=F32).astype(BF16)
    right = jnp.concatenate([window[b * taps : (b + 2) * taps] for b in range(blocks)], 1)
    lane_group = (lax.broadcasted_iota(jnp.int32, left.shape, 1) % LANES) // (LANES // groups)
    zero = jnp.zeros_like(left)
    stacked = jnp.concatenate([jnp.where(lane_group == g, left, zero) for g in range(groups)], 0)
    corr = lax.dot_general(stacked, right, (((1,), (1,)), ((), ())), preferred_element_type=F32)
    sums = [
        jnp.sum(
            pltpu.roll(corr[g * taps : (g + 1) * taps], 0, 1, stride=1, stride_axis=0),
            axis=0,
            keepdims=True,
        )[:, taps:]
        for g in range(groups)
    ]
    filter_ref[...] = jnp.concatenate(sums, 0)


def filter_part(inner, mixed, rim, group_count):
    tokens, width = inner.shape
    taps = rim.shape[0]
    groups = LANES * group_count // width
    column = pl.BlockSpec((tokens, LANES), lambda i: (0, i))
    return pl.pallas_call(
        functools.partial(filter_body, taps, groups),
        grid=(width // LANES,),
        in_specs=[column, column, pl.BlockSpec((taps, LANES), lambda i: (0, i))],
        out_specs=pl.BlockSpec((groups, taps), lambda i: (i, 0)),
        out_shape=jax.ShapeDtypeStruct((group_count, taps), F32),
        compiler_params=pltpu.CompilerParams(vmem_limit_bytes=32 * MIB),
        cost_estimate=LIGHT,
        name="filter_part",
    )(inner, mixed, rim)


def backward_body(taps, groups, rows_ref, inner_ref, ahead_ref, k_ref, v_ref, gk_ref, gv_ref):
    window = jnp.concatenate([inner_ref[...], ahead_ref[...]], 0)
    grad = banded(group_tables(rows_ref[...], 2 * taps), window, taps, groups)
    gk_ref[...] = (grad * v_ref[...].astype(F32)).astype(BF16)
    gv_ref[...] = (grad * k_ref[...].astype(F32)).astype(BF16)


def backward(rows, inner, ahead, k, v):
    tokens, width = k.shape
    taps = ahead.shape[0]
    groups = LANES * rows.shape[0] // width
    column = pl.BlockSpec((tokens, LANES), lambda i: (0, i))
    return pl.pallas_call(
        functools.partial(backward_body, taps, groups),
        grid=(width // LANES,),
        in_specs=[
            pl.BlockSpec((groups, 2 * taps), lambda i: (i, 0)),
            column,
            pl.BlockSpec((taps, LANES), lambda i: (0, i)),
            column,
            column,
        ],
        out_specs=[column, column],
        out_shape=[jax.ShapeDtypeStruct((tokens, width), BF16)] * 2,
        compiler_params=pltpu.CompilerParams(vmem_limit_bytes=24 * MIB),
        cost_estimate=LIGHT,
        name="conv_backward",
    )(rows, inner, ahead, k, v)


def sum_over(value, axis):
    count = lax.axis_size(axis)
    copies = jnp.broadcast_to(value[None], (count, *value.shape))
    return jnp.sum(lax.all_to_all(copies, axis, split_axis=0, concat_axis=0, tiled=True), 0)


def on_device(query_in, key_in, value_in, filters, proj_out, cotangent):
    tokens, width = query_in.shape
    group_count, taps = filters.shape
    half = width // 2
    x, y, c = (lax.axis_index(a) for a in ("x", "y", "c"))
    part = cotangent.shape[1] // 4

    proj = lax.all_gather(proj_out, "z", axis=0, tiled=True)

    rim = send_along_tokens(product(key_in[tokens - taps :], value_in[tokens - taps :]), 1)
    own_cols = lambda d: lax.dynamic_slice_in_dim(cotangent, ((x + d) % 4) * part, part, 1)
    pieces = [own_cols(0), None, None, None]
    for d in (2, 1, 3):
        pieces[(-d) % 4] = send(own_cols(d), "x", d)
    column = jnp.concatenate(pieces, 0)
    below, above = send(column, "y", 1), send(column, "y", -1)
    middle = column.shape[0] // 2
    far = send(below[:middle], "y", 1), send(above[middle:], "y", -1)

    taps32 = filters.astype(F32)
    rows = jnp.concatenate(
        [jnp.zeros((group_count, 1), F32), jnp.flip(taps32, 1), jnp.zeros((group_count, taps - 1), F32)], 1
    )
    back_rows = jnp.concatenate([taps32, jnp.zeros((group_count, taps), F32)], 1)
    conv, mixed, gated_a = forward(0, rows, key_in, value_in, query_in, rim, None)
    conv, mixed, gated_b = forward(1, rows, key_in, value_in, query_in, rim, (conv, mixed))
    left_a, right_b = send(gated_a, "x", 1), send(gated_b, "x", -1)
    right_a, left_b = send(gated_a, "x", -1), send(gated_b, "x", 1)
    far_a, far_b = send(left_a, "x", 1), send(right_b, "x", -1)
    gated = [gated_a, gated_b, right_a, right_b, far_a, far_b, left_a, left_b]

    far = after(far[0], left_a, right_b), far[1]
    mine = jnp.concatenate([column, above, *far, below], 0).reshape(4, 4 * tokens, part)
    sib = send(after(mine, right_a, left_b), "c", 1)
    place = jnp.stack([2 * ((y + dy) % 4) + (c if i == 0 else 1 - c) for dy in range(4) for i in range(2)])
    place = place.astype(jnp.int32)

    share = lambda d, h, dtype, *addends: gate_part(place, mine, sib, proj, d, h, dtype, *addends)
    far_a, far_b = send(share(2, 0, BF16), "x", 1), send(share(2, 1, BF16), "x", -1)
    proj = after(proj, *gated[4:6])
    early = share(1, 1, BF16), share(3, 0, BF16)
    from_left_b, from_right_a = send(early[0], "x", 1), send(early[1], "x", -1)
    gated[0] = after(gated[0], far_a, far_b, *early)
    proj_sums = proj_part(place, mine, sib, gated)
    grad_proj = lax.psum_scatter(proj_sums, "z", scatter_dimension=0, tiled=True).astype(F32)

    from_left_a = send(share(1, 0, BF16, far_a), "x", 1)
    from_right_b = send(share(3, 1, BF16, far_b), "x", -1)
    own = share(0, 0, F32), share(0, 1, F32)
    from_left, from_right = (from_left_a, from_left_b), (from_right_a, from_right_b)

    first = [
        (
            (own[h][:taps] + from_left[h][:taps].astype(F32) + from_right[h][:taps].astype(F32))
            * query_in[:taps, h * half : (h + 1) * half].astype(F32)
        ).astype(BF16)
        for h in range(2)
    ]
    first = jnp.concatenate(first, 1)
    ahead = send_along_tokens(first, -1)
    grad_query, inner = gate_gradients(
        (after(own[0], first), own[1]), from_left, from_right, query_in, conv
    )
    sums = filter_part(after(inner, ahead), mixed, rim, group_count)
    sums = sum_over(sums, "x")
    grad_key, grad_value = backward(back_rows, inner, ahead, key_in, value_in)
    grad_filter = jnp.flip(sum_over(sums, "z"), 1)
    return grad_query, grad_key, grad_value, grad_filter, grad_proj


def solution(mesh):
    ctx, tp = mesh.devices.shape
    shape = (ctx // SIZE["x"], SIZE["x"], tp // SIZE["c"], SIZE["c"])
    fine = Mesh(mesh.devices.reshape(shape), AXES)
    spec, along = P(("z", "x"), ("y", "c")), P(("y", "c"), None)
    return jax.shard_map(
        on_device,
        mesh=fine,
        in_specs=(spec, spec, spec, along, spec, spec),
        out_specs=(spec, spec, spec, along, spec),
        check_vma=False,
    )
```

```python
import functools

import jax
import jax.numpy as jnp
from jax import lax
from jax.experimental import pallas as pl
from jax.experimental.pallas import tpu as pltpu
from jax.sharding import Mesh
from jax.sharding import PartitionSpec as P

F32, BF16 = jnp.float32, jnp.bfloat16
LANES = 128
AXES = ("z", "x", "y", "c")
SIZE = {"x": 4, "y": 4, "c": 2}
MIB = 1 << 20
LIGHT = pl.CostEstimate(flops=1 << 20, bytes_accessed=1 << 18, transcendentals=0)


def send(value, axis, by):
    count = lax.axis_size(axis)
    return lax.ppermute(value, axis, [(i, (i + by) % count) for i in range(count)])


def send_along_tokens(value, by):
    count = lax.axis_size("z") * lax.axis_size("x")
    pairs = [(i, i + by) for i in range(count) if 0 <= i + by < count]
    return lax.ppermute(value, ("z", "x"), pairs)


def after(value, *others):
    return lax.optimization_barrier((value, *others))[0]


def product(a, b):
    return (a.astype(F32) * b.astype(F32)).astype(BF16)


def anti_identity(size):
    at = sum(lax.broadcasted_iota(jnp.int32, (size, size), i) for i in range(2))
    return (at == size - 1).astype(F32).astype(BF16)


def group_tables(filters, reverse):
    taps = filters.shape[1]
    if reverse:
        filters = jnp.dot(filters, anti_identity(taps), preferred_element_type=F32)
    rows = jnp.concatenate([filters.astype(F32), jnp.zeros(filters.shape, F32)], 1)
    tables = [
        pltpu.roll(
            jnp.broadcast_to(rows[g : g + 1], (taps, 2 * taps)), int(reverse), 1, stride=1, stride_axis=0
        )
        for g in range(rows.shape[0])
    ]
    return jnp.concatenate(tables, 0).astype(BF16)


def banded(tables, window, taps, groups):
    lane_group = lax.broadcasted_iota(jnp.int32, (taps, LANES), 1) // (LANES // groups)
    blocks = window.shape[0] // taps - 1
    out = []
    for b in range(0, blocks, 2):
        pair = jnp.concatenate(
            [window[(b + i) * taps : (b + i + 2) * taps] for i in range(2)], 1
        )
        res = jnp.dot(tables, pair, preferred_element_type=F32)
        for i in range(2):
            cols = slice(i * LANES, (i + 1) * LANES)
            acc = res[:taps, cols]
            for g in range(1, groups):
                acc = jnp.where(lane_group == g, res[g * taps : (g + 1) * taps, cols], acc)
            out.append(acc)
    return jnp.concatenate(out, 0)


def forward_body(taps, groups, filters_ref, k_ref, v_ref, q_ref, rim_ref, *refs):
    conv_ref, mixed_ref, gated_ref = refs[-3:]
    mixed = product(k_ref[...], v_ref[...])
    window = jnp.concatenate([rim_ref[...], mixed], 0)
    conv = banded(group_tables(filters_ref[...], True), window, taps, groups)
    conv_ref[...] = conv
    mixed_ref[...] = mixed
    gated_ref[...] = (q_ref[...].astype(F32) * conv).astype(BF16)


def forward(half, filters, k, v, q, rim, earlier):
    tokens, width = k.shape
    taps = rim.shape[0]
    groups = LANES * filters.shape[0] // width
    steps = width // LANES // 2
    at = lambda i: (0, i + half * steps)
    column = pl.BlockSpec((tokens, LANES), at)
    in_specs = [
        pl.BlockSpec((groups, taps), lambda i: (i + half * steps, 0)),
        column,
        column,
        column,
        pl.BlockSpec((taps, LANES), at),
    ]
    args = [filters, k, v, q, rim]
    aliases = {}
    if earlier is not None:
        in_specs += [pl.BlockSpec(memory_space=pl.ANY)] * 2
        args += list(earlier)
        aliases = {5: 0, 6: 1}
    return pl.pallas_call(
        functools.partial(forward_body, taps, groups),
        grid=(steps,),
        in_specs=in_specs,
        out_specs=[column, column, pl.BlockSpec((tokens, LANES), lambda i: (0, i))],
        out_shape=[
            jax.ShapeDtypeStruct((tokens, width), F32),
            jax.ShapeDtypeStruct((tokens, width), BF16),
            jax.ShapeDtypeStruct((tokens, width // 2), BF16),
        ],
        input_output_aliases=aliases,
        compiler_params=pltpu.CompilerParams(vmem_limit_bytes=16 * MIB),
        cost_estimate=LIGHT,
        name="conv_forward",
    )(*args)


def gate_body(place_ref, mine_ref, sib_ref, proj_ref, *refs):
    added, outs = refs[:-2], refs[-2:]
    rows = proj_ref.shape[0] // 8
    acc = None
    for dy in range(4):
        lhs = jnp.concatenate([mine_ref[dy], sib_ref[dy]], 1)
        rhs = jnp.concatenate(
            [
                proj_ref[pl.ds(pl.multiple_of(place_ref[2 * dy + i] * rows, rows), rows), :]
                for i in range(2)
            ],
            0,
        )
        term = jnp.dot(lhs, rhs, preferred_element_type=F32)
        acc = term if acc is None else acc + term
    second = pl.program_id(0) >= pl.num_programs(0) // 2
    if added:
        acc = acc + jnp.where(second, added[1][...], added[0][...]).astype(F32)
    acc = acc.astype(outs[0].dtype)

    @pl.when(jnp.logical_not(second))
    def _():
        outs[0][...] = acc

    @pl.when(second)
    def _():
        outs[1][...] = acc


def gate_parts(place, mine, sib, proj, wanted, dtype, *added):
    depth, width = proj.shape
    tokens = mine.shape[1] // 4
    tile = 256
    steps = width // 2 // tile
    (block0, half0), (block1, half1) = wanted
    choose = lambda i, first, second: jnp.where(i < steps, first, second)
    cot = pl.BlockSpec((4, tokens, depth // 8), lambda i, p: (0, choose(i, block0, block1), 0))
    pair = [
        pl.BlockSpec((tokens, tile), lambda i, p: (0, jnp.minimum(i, steps - 1))),
        pl.BlockSpec((tokens, tile), lambda i, p: (0, jnp.maximum(i - steps, 0))),
    ]
    spec = pltpu.PrefetchScalarGridSpec(
        num_scalar_prefetch=1,
        grid=(2 * steps,),
        in_specs=[
            cot,
            cot,
            pl.BlockSpec((depth, tile), lambda i, p: (0, i % steps + choose(i, half0, half1) * steps)),
        ]
        + pair[: len(added)],
        out_specs=pair,
    )
    return pl.pallas_call(
        gate_body,
        grid_spec=spec,
        out_shape=[jax.ShapeDtypeStruct((tokens, width // 2), dtype)] * 2,
        compiler_params=pltpu.CompilerParams(vmem_limit_bytes=16 * MIB),
        cost_estimate=LIGHT,
        name="grad_gate_parts",
    )(place, mine, sib, proj, *added)


def proj_body(place_ref, mine_ref, sib_ref, *refs):
    gated_refs, out_ref = refs[:-1], refs[-1]
    rows = mine_ref.shape[1]
    tokens, half = gated_refs[0].shape
    core = place_ref[0] % 2
    for h in range(2):
        acc = None
        for d in range(4):
            at = pl.ds(d * tokens, tokens)
            lhs = jnp.concatenate([mine_ref[at, :], sib_ref[at, :]], 1)
            term = lax.dot_general(
                lhs, gated_refs[2 * d + h][...], (((0,), (0,)), ((), ())), preferred_element_type=F32
            )
            acc = term if acc is None else acc + term
        acc = acc.astype(BF16)
        cols = pl.ds(h * half, half)
        out_ref[pl.ds(pl.multiple_of(core * rows, rows), rows), cols] = acc[:rows]
        out_ref[pl.ds(pl.multiple_of((1 - core) * rows, rows), rows), cols] = acc[rows:]


def proj_part(place, mine, sib, gated):
    rows = mine.shape[2]
    depth = 8 * rows
    tokens, half = gated[0].shape
    spec = pltpu.PrefetchScalarGridSpec(
        num_scalar_prefetch=1,
        grid=(4,),
        in_specs=[pl.BlockSpec((None, 4 * tokens, rows), lambda i, p: (i, 0, 0))] * 2
        + [pl.BlockSpec((tokens, half), lambda i, p: (0, 0))] * 8,
        out_specs=pl.BlockSpec((2 * rows, 2 * half), lambda i, p: (p[2 * i] // 2, 0)),
    )
    return pl.pallas_call(
        proj_body,
        grid_spec=spec,
        out_shape=jax.ShapeDtypeStruct((depth, 2 * half), BF16),
        compiler_params=pltpu.CompilerParams(vmem_limit_bytes=24 * MIB),
        cost_estimate=LIGHT,
        name="grad_proj_part",
    )(place, mine, sib, *gated)


def inner_body(*refs):
    own, from_left, from_right = refs[0:2], refs[2:4], refs[4:6]
    q_ref, conv_ref, query_ref, inner_ref = refs[6:]
    second = pl.program_id(0) >= pl.num_programs(0) // 2
    pick = lambda pair: jnp.where(second, pair[1][...], pair[0][...]).astype(F32)
    gate = pick(own) + pick(from_left) + pick(from_right)
    query_ref[...] = (gate * conv_ref[...]).astype(BF16)
    inner_ref[...] = (gate * q_ref[...].astype(F32)).astype(BF16)


def gate_gradients(own, from_left, from_right, q, conv):
    tokens, width = q.shape
    wide = 2 * LANES
    steps = width // wide
    column = pl.BlockSpec((tokens, wide), lambda i: (0, i))
    first = pl.BlockSpec((tokens, wide), lambda i: (0, jnp.minimum(i, steps // 2 - 1)))
    last = pl.BlockSpec((tokens, wide), lambda i: (0, jnp.maximum(i - steps // 2, 0)))
    return pl.pallas_call(
        inner_body,
        grid=(steps,),
        in_specs=[first, last] * 3 + [column, column],
        out_specs=[column, column],
        out_shape=[jax.ShapeDtypeStruct((tokens, width), BF16)] * 2,
        compiler_params=pltpu.CompilerParams(vmem_limit_bytes=16 * MIB),
        cost_estimate=LIGHT,
        name="gate_gradients",
    )(*own, *from_left, *from_right, q, conv)


def filter_body(taps, groups, inner_ref, mixed_ref, rim_ref, filter_ref):
    inner = inner_ref[...]
    window = jnp.concatenate([rim_ref[...], mixed_ref[...]], 0)
    blocks = inner.shape[0] // taps
    left = jnp.concatenate([inner[b * taps : (b + 1) * taps] for b in range(blocks)], 1)
    left = jnp.dot(anti_identity(taps), left, preferred_element_type=F32).astype(BF16)
    right = jnp.concatenate([window[b * taps : (b + 2) * taps] for b in range(blocks)], 1)
    lane_group = (lax.broadcasted_iota(jnp.int32, left.shape, 1) % LANES) // (LANES // groups)
    zero = jnp.zeros_like(left)
    stacked = jnp.concatenate([jnp.where(lane_group == g, left, zero) for g in range(groups)], 0)
    corr = lax.dot_general(stacked, right, (((1,), (1,)), ((), ())), preferred_element_type=F32)
    sums = [
        jnp.sum(
            pltpu.roll(corr[g * taps : (g + 1) * taps], 0, 1, stride=1, stride_axis=0),
            axis=0,
            keepdims=True,
        )[:, taps:]
        for g in range(groups)
    ]
    filter_ref[...] = jnp.concatenate(sums, 0)


def filter_part(inner, mixed, rim, group_count):
    tokens, width = inner.shape
    taps = rim.shape[0]
    groups = LANES * group_count // width
    column = pl.BlockSpec((tokens, LANES), lambda i: (0, i))
    return pl.pallas_call(
        functools.partial(filter_body, taps, groups),
        grid=(width // LANES,),
        in_specs=[column, column, pl.BlockSpec((taps, LANES), lambda i: (0, i))],
        out_specs=pl.BlockSpec((groups, taps), lambda i: (i, 0)),
        out_shape=jax.ShapeDtypeStruct((group_count, taps), F32),
        compiler_params=pltpu.CompilerParams(vmem_limit_bytes=16 * MIB),
        cost_estimate=LIGHT,
        name="filter_part",
    )(inner, mixed, rim)


def backward_body(taps, groups, filters_ref, inner_ref, ahead_ref, k_ref, v_ref, gk_ref, gv_ref):
    window = jnp.concatenate([inner_ref[...], ahead_ref[...]], 0)
    grad = banded(group_tables(filters_ref[...], False), window, taps, groups)
    gk_ref[...] = (grad * v_ref[...].astype(F32)).astype(BF16)
    gv_ref[...] = (grad * k_ref[...].astype(F32)).astype(BF16)


def backward(filters, inner, ahead, k, v):
    tokens, width = k.shape
    taps = ahead.shape[0]
    groups = LANES * filters.shape[0] // width
    column = pl.BlockSpec((tokens, LANES), lambda i: (0, i))
    return pl.pallas_call(
        functools.partial(backward_body, taps, groups),
        grid=(width // LANES,),
        in_specs=[
            pl.BlockSpec((groups, taps), lambda i: (i, 0)),
            column,
            pl.BlockSpec((taps, LANES), lambda i: (0, i)),
            column,
            column,
        ],
        out_specs=[column, column],
        out_shape=[jax.ShapeDtypeStruct((tokens, width), BF16)] * 2,
        compiler_params=pltpu.CompilerParams(vmem_limit_bytes=16 * MIB),
        cost_estimate=LIGHT,
        name="conv_backward",
    )(filters, inner, ahead, k, v)


def sum_over(value, axis, *beside):
    count, me = lax.axis_size(axis), lax.axis_index(axis)
    terms = [after(value, *beside)] + [send(value, axis, d) for d in range(1, count)]
    total = None
    for source in range(count):
        term = terms[0]
        for d in range(1, count):
            term = jnp.where((me - source) % count == d, terms[d], term)
        total = term if total is None else total + term
    return total


def on_device(query_in, key_in, value_in, filters, proj_out, cotangent):
    tokens, width = query_in.shape
    group_count, taps = filters.shape
    half = width // 2
    x, y, c = (lax.axis_index(a) for a in ("x", "y", "c"))
    part = cotangent.shape[1] // 4

    proj = lax.all_gather(proj_out, "z", axis=0, tiled=True)

    last = product(key_in[tokens - taps :], value_in[tokens - taps :])
    rim = send_along_tokens(last, 1)
    base = after(x, last)
    own_cols = lambda d: lax.dynamic_slice_in_dim(cotangent, ((base + d) % 4) * part, part, 1)
    pieces = [own_cols(0), None, None, None]
    for d in (2, 1, 3):
        pieces[(-d) % 4] = send(own_cols(d), "x", d)
    column = jnp.concatenate([after(pieces[0], rim), *pieces[1:]], 0)
    below, above = send(column, "y", 1), send(column, "y", -1)
    middle = column.shape[0] // 2
    far = send(below[:middle], "y", 1), send(above[middle:], "y", -1)

    conv, mixed, gated_a = forward(0, filters, key_in, value_in, query_in, rim, None)
    conv, mixed, gated_b = forward(1, filters, key_in, value_in, query_in, rim, (conv, mixed))
    left_a, right_b = send(gated_a, "x", 1), send(gated_b, "x", -1)
    right_a, left_b = send(gated_a, "x", -1), send(gated_b, "x", 1)
    far_a, far_b = send(left_a, "x", 1), send(right_b, "x", -1)
    gated = [gated_a, gated_b, right_a, right_b, far_a, far_b, left_a, left_b]

    far = after(far[0], left_a, right_b), far[1]
    mine = jnp.concatenate([column, above, *far, below], 0).reshape(4, 4 * tokens, part)
    sib = send(after(mine, right_a, left_b), "c", 1)
    place = jnp.stack([2 * ((y + dy) % 4) + (c if i == 0 else 1 - c) for dy in range(4) for i in range(2)])
    place = place.astype(jnp.int32)

    across = gate_parts(place, mine, sib, proj, ((2, 0), (2, 1)), BF16)
    far_a, far_b = send(across[0], "x", 1), send(across[1], "x", -1)
    proj = after(proj, *across, *gated[4:6])
    beside = gate_parts(place, mine, sib, proj, ((1, 1), (3, 0)), BF16)
    from_left_b, from_right_a = send(beside[0], "x", 1), send(beside[1], "x", -1)
    gated[0] = after(gated[0], *beside)
    proj_sums = proj_part(place, mine, sib, gated)
    proj_sums = after(proj_sums, far_a, far_b)
    grad_proj = lax.psum_scatter(proj_sums, "z", scatter_dimension=0, tiled=True).astype(F32)

    joined = gate_parts(place, mine, sib, proj, ((1, 0), (3, 1)), BF16, far_a, far_b)
    from_left_a, from_right_b = send(joined[0], "x", 1), send(joined[1], "x", -1)
    own = gate_parts(place, mine, sib, proj, ((0, 0), (0, 1)), F32)
    from_left, from_right = (from_left_a, from_left_b), (from_right_a, from_right_b)

    first = [
        (
            (own[h][:taps] + from_left[h][:taps].astype(F32) + from_right[h][:taps].astype(F32))
            * query_in[:taps, h * half : (h + 1) * half].astype(F32)
        ).astype(BF16)
        for h in range(2)
    ]
    first = jnp.concatenate(first, 1)
    ahead = send_along_tokens(first, -1)
    grad_query, inner = gate_gradients(
        (after(own[0], first), own[1]), from_left, from_right, query_in, conv
    )
    sums = filter_part(inner, mixed, rim, group_count)
    grad_key, grad_value = backward(filters, after(inner, sums), ahead, key_in, value_in)
    sums = sum_over(sums, "x", grad_key)
    grad_filter = jnp.flip(sum_over(sums, "z"), 1)
    return grad_query, grad_key, grad_value, grad_filter, grad_proj


def solution(mesh):
    ctx, tp = mesh.devices.shape
    shape = (ctx // SIZE["x"], SIZE["x"], tp // SIZE["c"], SIZE["c"])
    fine = Mesh(mesh.devices.reshape(shape), AXES)
    spec, along = P(("z", "x"), ("y", "c")), P(("y", "c"), None)
    return jax.shard_map(
        on_device,
        mesh=fine,
        in_specs=(spec, spec, spec, along, spec, spec),
        out_specs=(spec, spec, spec, along, spec),
        check_vma=False,
    )
```

```python
import functools

import jax
import jax.numpy as jnp
from jax import lax
from jax.experimental import pallas as pl
from jax.experimental.pallas import tpu as pltpu
from jax.sharding import Mesh
from jax.sharding import PartitionSpec as P

F32, BF16 = jnp.float32, jnp.bfloat16
LANES = 128
AXES = ("z", "x", "y", "c")
SIZE = {"x": 4, "y": 4, "c": 2}
MIB = 1 << 20
LIGHT = pl.CostEstimate(flops=1 << 20, bytes_accessed=1 << 18, transcendentals=0)


def send(value, axis, by):
    count = lax.axis_size(axis)
    return lax.ppermute(value, axis, [(i, (i + by) % count) for i in range(count)])


def send_along_tokens(value, by):
    count = lax.axis_size("z") * lax.axis_size("x")
    pairs = [(i, i + by) for i in range(count) if 0 <= i + by < count]
    return lax.ppermute(value, ("z", "x"), pairs)


def after(value, *others):
    return lax.optimization_barrier((value, *others))[0]


def product(a, b):
    return (a.astype(F32) * b.astype(F32)).astype(BF16)


def anti_identity(size):
    at = sum(lax.broadcasted_iota(jnp.int32, (size, size), i) for i in range(2))
    return (at == size - 1).astype(F32).astype(BF16)


def group_tables(filters, reverse):
    taps = filters.shape[1]
    if reverse:
        filters = jnp.dot(filters, anti_identity(taps), preferred_element_type=F32)
    rows = jnp.concatenate([filters.astype(F32), jnp.zeros(filters.shape, F32)], 1)
    tables = [
        pltpu.roll(
            jnp.broadcast_to(rows[g : g + 1], (taps, 2 * taps)), int(reverse), 1, stride=1, stride_axis=0
        )
        for g in range(rows.shape[0])
    ]
    return jnp.concatenate(tables, 0).astype(BF16)


def banded(tables, window, taps, groups):
    lane_group = lax.broadcasted_iota(jnp.int32, (taps, LANES), 1) // (LANES // groups)
    blocks = window.shape[0] // taps - 1
    out = []
    for b in range(0, blocks, 2):
        pair = jnp.concatenate(
            [window[(b + i) * taps : (b + i + 2) * taps] for i in range(2)], 1
        )
        res = jnp.dot(tables, pair, preferred_element_type=F32)
        for i in range(2):
            cols = slice(i * LANES, (i + 1) * LANES)
            acc = res[:taps, cols]
            for g in range(1, groups):
                acc = jnp.where(lane_group == g, res[g * taps : (g + 1) * taps, cols], acc)
            out.append(acc)
    return jnp.concatenate(out, 0)


def forward_body(taps, groups, filters_ref, k_ref, v_ref, q_ref, rim_ref, *refs):
    conv_ref, mixed_ref, gated_ref = refs[-3:]
    mixed = product(k_ref[...], v_ref[...])
    window = jnp.concatenate([rim_ref[...], mixed], 0)
    conv = banded(group_tables(filters_ref[...], True), window, taps, groups)
    conv_ref[...] = conv
    mixed_ref[...] = mixed
    gated_ref[...] = (q_ref[...].astype(F32) * conv).astype(BF16)


def forward(half, filters, k, v, q, rim, earlier):
    tokens, width = k.shape
    taps = rim.shape[0]
    groups = LANES * filters.shape[0] // width
    steps = width // LANES // 2
    at = lambda i: (0, i + half * steps)
    column = pl.BlockSpec((tokens, LANES), at)
    in_specs = [
        pl.BlockSpec((groups, taps), lambda i: (i + half * steps, 0)),
        column,
        column,
        column,
        pl.BlockSpec((taps, LANES), at),
    ]
    args = [filters, k, v, q, rim]
    aliases = {}
    if earlier is not None:
        in_specs += [pl.BlockSpec(memory_space=pl.ANY)] * 2
        args += list(earlier)
        aliases = {5: 0, 6: 1}
    return pl.pallas_call(
        functools.partial(forward_body, taps, groups),
        grid=(steps,),
        in_specs=in_specs,
        out_specs=[column, column, pl.BlockSpec((tokens, LANES), lambda i: (0, i))],
        out_shape=[
            jax.ShapeDtypeStruct((tokens, width), F32),
            jax.ShapeDtypeStruct((tokens, width), BF16),
            jax.ShapeDtypeStruct((tokens, width // 2), BF16),
        ],
        input_output_aliases=aliases,
        compiler_params=pltpu.CompilerParams(vmem_limit_bytes=16 * MIB),
        cost_estimate=LIGHT,
        name="conv_forward",
    )(*args)


def gate_body(place_ref, mine_ref, sib_ref, proj_ref, *refs):
    added, outs = refs[:-2], refs[-2:]
    rows = proj_ref.shape[0] // 8
    acc = None
    for dy in range(4):
        lhs = jnp.concatenate([mine_ref[dy], sib_ref[dy]], 1)
        rhs = jnp.concatenate(
            [
                proj_ref[pl.ds(pl.multiple_of(place_ref[2 * dy + i] * rows, rows), rows), :]
                for i in range(2)
            ],
            0,
        )
        term = jnp.dot(lhs, rhs, preferred_element_type=F32)
        acc = term if acc is None else acc + term
    second = pl.program_id(0) >= pl.num_programs(0) // 2
    if added:
        acc = acc + jnp.where(second, added[1][...], added[0][...]).astype(F32)
    acc = acc.astype(outs[0].dtype)

    @pl.when(jnp.logical_not(second))
    def _():
        outs[0][...] = acc

    @pl.when(second)
    def _():
        outs[1][...] = acc


def gate_parts(place, mine, sib, proj, wanted, dtype, *added):
    depth, width = proj.shape
    tokens = mine.shape[1] // 4
    tile = 256
    steps = width // 2 // tile
    (block0, half0), (block1, half1) = wanted
    choose = lambda i, first, second: jnp.where(i < steps, first, second)
    cot = pl.BlockSpec((4, tokens, depth // 8), lambda i, p: (0, choose(i, block0, block1), 0))
    pair = [
        pl.BlockSpec((tokens, tile), lambda i, p: (0, jnp.minimum(i, steps - 1))),
        pl.BlockSpec((tokens, tile), lambda i, p: (0, jnp.maximum(i - steps, 0))),
    ]
    spec = pltpu.PrefetchScalarGridSpec(
        num_scalar_prefetch=1,
        grid=(2 * steps,),
        in_specs=[
            cot,
            cot,
            pl.BlockSpec((depth, tile), lambda i, p: (0, i % steps + choose(i, half0, half1) * steps)),
        ]
        + pair[: len(added)],
        out_specs=pair,
    )
    return pl.pallas_call(
        gate_body,
        grid_spec=spec,
        out_shape=[jax.ShapeDtypeStruct((tokens, width // 2), dtype)] * 2,
        compiler_params=pltpu.CompilerParams(vmem_limit_bytes=16 * MIB),
        cost_estimate=LIGHT,
        name="grad_gate_parts",
    )(place, mine, sib, proj, *added)


def proj_body(place_ref, mine_ref, sib_ref, *refs):
    gated_refs, out_ref = refs[:-1], refs[-1]
    rows = mine_ref.shape[1]
    tokens, half = gated_refs[0].shape
    core = place_ref[0] % 2
    for h in range(2):
        acc = None
        for d in range(4):
            at = pl.ds(d * tokens, tokens)
            lhs = jnp.concatenate([mine_ref[at, :], sib_ref[at, :]], 1)
            term = lax.dot_general(
                lhs, gated_refs[2 * d + h][...], (((0,), (0,)), ((), ())), preferred_element_type=F32
            )
            acc = term if acc is None else acc + term
        acc = acc.astype(BF16)
        cols = pl.ds(h * half, half)
        out_ref[pl.ds(pl.multiple_of(core * rows, rows), rows), cols] = acc[:rows]
        out_ref[pl.ds(pl.multiple_of((1 - core) * rows, rows), rows), cols] = acc[rows:]


def proj_part(place, mine, sib, gated):
    rows = mine.shape[2]
    depth = 8 * rows
    tokens, half = gated[0].shape
    spec = pltpu.PrefetchScalarGridSpec(
        num_scalar_prefetch=1,
        grid=(4,),
        in_specs=[pl.BlockSpec((None, 4 * tokens, rows), lambda i, p: (i, 0, 0))] * 2
        + [pl.BlockSpec((tokens, half), lambda i, p: (0, 0))] * 8,
        out_specs=pl.BlockSpec((2 * rows, 2 * half), lambda i, p: (p[2 * i] // 2, 0)),
    )
    return pl.pallas_call(
        proj_body,
        grid_spec=spec,
        out_shape=jax.ShapeDtypeStruct((depth, 2 * half), BF16),
        compiler_params=pltpu.CompilerParams(vmem_limit_bytes=24 * MIB),
        cost_estimate=LIGHT,
        name="grad_proj_part",
    )(place, mine, sib, *gated)


def inner_body(*refs):
    own, from_left, from_right = refs[0:2], refs[2:4], refs[4:6]
    q_ref, conv_ref, query_ref, inner_ref = refs[6:]
    second = pl.program_id(0) >= pl.num_programs(0) // 2
    pick = lambda pair: jnp.where(second, pair[1][...], pair[0][...]).astype(F32)
    gate = pick(own) + pick(from_left) + pick(from_right)
    query_ref[...] = (gate * conv_ref[...]).astype(BF16)
    inner_ref[...] = (gate * q_ref[...].astype(F32)).astype(BF16)


def gate_gradients(own, from_left, from_right, q, conv):
    tokens, width = q.shape
    wide = 2 * LANES
    steps = width // wide
    column = pl.BlockSpec((tokens, wide), lambda i: (0, i))
    first = pl.BlockSpec((tokens, wide), lambda i: (0, jnp.minimum(i, steps // 2 - 1)))
    last = pl.BlockSpec((tokens, wide), lambda i: (0, jnp.maximum(i - steps // 2, 0)))
    return pl.pallas_call(
        inner_body,
        grid=(steps,),
        in_specs=[first, last] * 3 + [column, column],
        out_specs=[column, column],
        out_shape=[jax.ShapeDtypeStruct((tokens, width), BF16)] * 2,
        compiler_params=pltpu.CompilerParams(vmem_limit_bytes=16 * MIB),
        cost_estimate=LIGHT,
        name="gate_gradients",
    )(*own, *from_left, *from_right, q, conv)


def filter_body(taps, groups, inner_ref, mixed_ref, rim_ref, filter_ref):
    inner = inner_ref[...]
    window = jnp.concatenate([rim_ref[...], mixed_ref[...]], 0)
    blocks = inner.shape[0] // taps
    left = jnp.concatenate([inner[b * taps : (b + 1) * taps] for b in range(blocks)], 1)
    left = jnp.dot(anti_identity(taps), left, preferred_element_type=F32).astype(BF16)
    right = jnp.concatenate([window[b * taps : (b + 2) * taps] for b in range(blocks)], 1)
    lane_group = (lax.broadcasted_iota(jnp.int32, left.shape, 1) % LANES) // (LANES // groups)
    zero = jnp.zeros_like(left)
    stacked = jnp.concatenate([jnp.where(lane_group == g, left, zero) for g in range(groups)], 0)
    corr = lax.dot_general(stacked, right, (((1,), (1,)), ((), ())), preferred_element_type=F32)
    sums = [
        jnp.sum(
            pltpu.roll(corr[g * taps : (g + 1) * taps], 0, 1, stride=1, stride_axis=0),
            axis=0,
            keepdims=True,
        )[:, taps:]
        for g in range(groups)
    ]
    turn = anti_identity(taps).astype(F32)
    filter_ref[...] = jnp.dot(
        jnp.concatenate(sums, 0), turn, precision=lax.Precision.HIGHEST, preferred_element_type=F32
    )


def filter_part(inner, mixed, rim, group_count):
    tokens, width = inner.shape
    taps = rim.shape[0]
    groups = LANES * group_count // width
    column = pl.BlockSpec((tokens, LANES), lambda i: (0, i))
    return pl.pallas_call(
        functools.partial(filter_body, taps, groups),
        grid=(width // LANES,),
        in_specs=[column, column, pl.BlockSpec((taps, LANES), lambda i: (0, i))],
        out_specs=pl.BlockSpec((groups, taps), lambda i: (i, 0)),
        out_shape=jax.ShapeDtypeStruct((group_count, taps), F32),
        compiler_params=pltpu.CompilerParams(vmem_limit_bytes=16 * MIB),
        cost_estimate=LIGHT,
        name="filter_part",
    )(inner, mixed, rim)


def backward_body(taps, groups, filters_ref, inner_ref, ahead_ref, k_ref, v_ref, gk_ref, gv_ref):
    window = jnp.concatenate([inner_ref[...], ahead_ref[...]], 0)
    grad = banded(group_tables(filters_ref[...], False), window, taps, groups)
    gk_ref[...] = (grad * v_ref[...].astype(F32)).astype(BF16)
    gv_ref[...] = (grad * k_ref[...].astype(F32)).astype(BF16)


def backward(filters, inner, ahead, k, v):
    tokens, width = k.shape
    taps = ahead.shape[0]
    groups = LANES * filters.shape[0] // width
    column = pl.BlockSpec((tokens, LANES), lambda i: (0, i))
    return pl.pallas_call(
        functools.partial(backward_body, taps, groups),
        grid=(width // LANES,),
        in_specs=[
            pl.BlockSpec((groups, taps), lambda i: (i, 0)),
            column,
            pl.BlockSpec((taps, LANES), lambda i: (0, i)),
            column,
            column,
        ],
        out_specs=[column, column],
        out_shape=[jax.ShapeDtypeStruct((tokens, width), BF16)] * 2,
        compiler_params=pltpu.CompilerParams(vmem_limit_bytes=16 * MIB),
        cost_estimate=LIGHT,
        name="conv_backward",
    )(filters, inner, ahead, k, v)


def sum_over(value, axis, stride, *beside):
    count, me = lax.axis_size(axis) // stride, lax.axis_index(axis) // stride
    terms = [after(value, *beside)] + [send(value, axis, d * stride) for d in range(1, count)]
    total = None
    for source in range(count):
        term = terms[0]
        for d in range(1, count):
            term = jnp.where((me - source) % count == d, terms[d], term)
        total = term if total is None else total + term
    return total


def on_device(query_in, key_in, value_in, filters, proj_out, cotangent):
    tokens, width = query_in.shape
    group_count, taps = filters.shape
    half = width // 2
    x, y, c = (lax.axis_index(a) for a in ("x", "y", "c"))
    part = cotangent.shape[1] // 4

    proj = lax.all_gather(proj_out, "z", axis=0, tiled=True)

    last = product(key_in[tokens - taps :], value_in[tokens - taps :])
    rim = send_along_tokens(last, 1)
    base = after(x, last)
    own_cols = lambda d: lax.dynamic_slice_in_dim(cotangent, ((base + d) % 4) * part, part, 1)
    pieces = [own_cols(0), None, None, None]
    for d in (2, 1, 3):
        pieces[(-d) % 4] = send(own_cols(d), "x", d)
    conv, mixed, gated_a = forward(0, filters, key_in, value_in, query_in, rim, None)
    conv, mixed, gated_b = forward(1, filters, key_in, value_in, query_in, rim, (conv, mixed))
    column = after(jnp.concatenate(pieces, 0), gated_a)
    below, above = send(column, "y", 1), send(column, "y", -1)
    middle = column.shape[0] // 2
    far = send(below[:middle], "y", 1), send(above[middle:], "y", -1)
    left_a, right_a = send(gated_a, "x", 1), send(gated_a, "x", -1)
    right_b, left_b = send(gated_b, "x", -1), send(after(gated_b, left_a, right_a), "x", 1)
    far_a, far_b = send(left_a, "x", 1), send(right_b, "x", -1)
    gated = [gated_a, gated_b, right_a, right_b, far_a, far_b, left_a, left_b]

    far = after(far[0], left_a, right_b), far[1]
    mine = jnp.concatenate([column, above, *far, below], 0).reshape(4, 4 * tokens, part)
    sib = send(after(mine, right_a, left_b), "c", 1)
    place = jnp.stack([2 * ((y + dy) % 4) + (c if i == 0 else 1 - c) for dy in range(4) for i in range(2)])
    place = place.astype(jnp.int32)

    across = gate_parts(place, mine, sib, proj, ((2, 0), (2, 1)), BF16)
    far_a, far_b = send(across[0], "x", 1), send(across[1], "x", -1)
    proj = after(proj, *across, *gated[4:6])
    beside = gate_parts(place, mine, sib, proj, ((1, 1), (3, 0)), BF16)
    from_left_b, from_right_a = send(beside[0], "x", 1), send(beside[1], "x", -1)
    gated[0] = after(gated[0], *beside)
    proj_sums = proj_part(place, mine, sib, gated)
    proj_sums = after(proj_sums, far_a, far_b)
    grad_proj = lax.psum_scatter(proj_sums, "z", scatter_dimension=0, tiled=True).astype(F32)

    joined = gate_parts(place, mine, sib, proj, ((1, 0), (3, 1)), BF16, far_a, far_b)
    from_left_a, from_right_b = send(joined[0], "x", 1), send(joined[1], "x", -1)
    own = gate_parts(place, mine, sib, proj, ((0, 0), (0, 1)), F32)
    from_left, from_right = (from_left_a, from_left_b), (from_right_a, from_right_b)

    first = [
        (
            (own[h][:taps] + from_left[h][:taps].astype(F32) + from_right[h][:taps].astype(F32))
            * query_in[:taps, h * half : (h + 1) * half].astype(F32)
        ).astype(BF16)
        for h in range(2)
    ]
    first = jnp.concatenate(first, 1)
    ahead = send_along_tokens(first, -1)
    grad_query, inner = gate_gradients(
        (after(own[0], first), own[1]), from_left, from_right, query_in, conv
    )
    sums = filter_part(inner, mixed, rim, group_count)
    grad_key, grad_value = backward(filters, after(inner, sums), ahead, key_in, value_in)
    sums = sum_over(sum_over(sums, "x", 1, grad_key), "z", 2)
    odd = lax.ppermute(sums, "z", [(i, i ^ 1) for i in range(lax.axis_size("z"))])
    grad_filter = after(sums, grad_proj) + odd
    return grad_query, grad_key, grad_value, grad_filter, grad_proj


def solution(mesh):
    ctx, tp = mesh.devices.shape
    shape = (ctx // SIZE["x"], SIZE["x"], tp // SIZE["c"], SIZE["c"])
    fine = Mesh(mesh.devices.reshape(shape), AXES)
    spec, along = P(("z", "x"), ("y", "c")), P(("y", "c"), None)
    return jax.shard_map(
        on_device,
        mesh=fine,
        in_specs=(spec, spec, spec, along, spec, spec),
        out_specs=(spec, spec, spec, along, spec),
        check_vma=False,
    )
```

```python
import functools

import jax
import jax.numpy as jnp
from jax import lax
from jax.experimental import pallas as pl
from jax.experimental.pallas import tpu as pltpu
from jax.sharding import Mesh
from jax.sharding import PartitionSpec as P

F32, BF16 = jnp.float32, jnp.bfloat16
LANES = 128
AXES = ("z", "x", "y", "c")
SIZE = {"x": 4, "y": 4, "c": 2}
MIB = 1 << 20
LIGHT = pl.CostEstimate(flops=1 << 20, bytes_accessed=1 << 18, transcendentals=0)


def send(value, axis, by):
    count = lax.axis_size(axis)
    return lax.ppermute(value, axis, [(i, (i + by) % count) for i in range(count)])


def send_along_tokens(value, by):
    count = lax.axis_size("z") * lax.axis_size("x")
    pairs = [(i, i + by) for i in range(count) if 0 <= i + by < count]
    return lax.ppermute(value, ("z", "x"), pairs)


def after(value, *others):
    return lax.optimization_barrier((value, *others))[0]


def product(a, b):
    return (a.astype(F32) * b.astype(F32)).astype(BF16)


def anti_identity(size):
    at = sum(lax.broadcasted_iota(jnp.int32, (size, size), i) for i in range(2))
    return (at == size - 1).astype(F32).astype(BF16)


def group_tables(filters, reverse):
    taps = filters.shape[1]
    if reverse:
        filters = jnp.dot(filters, anti_identity(taps), preferred_element_type=F32)
    rows = jnp.concatenate([filters.astype(F32), jnp.zeros(filters.shape, F32)], 1)
    tables = [
        pltpu.roll(
            jnp.broadcast_to(rows[g : g + 1], (taps, 2 * taps)), int(reverse), 1, stride=1, stride_axis=0
        )
        for g in range(rows.shape[0])
    ]
    return jnp.concatenate(tables, 0).astype(BF16)


def banded(tables, window, taps, groups):
    lane_group = lax.broadcasted_iota(jnp.int32, (taps, LANES), 1) // (LANES // groups)
    blocks = window.shape[0] // taps - 1
    out = []
    for b in range(0, blocks, 2):
        pair = jnp.concatenate(
            [window[(b + i) * taps : (b + i + 2) * taps] for i in range(2)], 1
        )
        res = jnp.dot(tables, pair, preferred_element_type=F32)
        for i in range(2):
            cols = slice(i * LANES, (i + 1) * LANES)
            acc = res[:taps, cols]
            for g in range(1, groups):
                acc = jnp.where(lane_group == g, res[g * taps : (g + 1) * taps, cols], acc)
            out.append(acc)
    return jnp.concatenate(out, 0)


def forward_body(taps, groups, filters_ref, k_ref, v_ref, q_ref, rim_ref, *refs):
    conv_ref, mixed_ref, gated_ref = refs[-3:]
    mixed = product(k_ref[...], v_ref[...])
    window = jnp.concatenate([rim_ref[...], mixed], 0)
    conv = banded(group_tables(filters_ref[...], True), window, taps, groups)
    conv_ref[...] = conv
    mixed_ref[...] = mixed
    gated_ref[...] = (q_ref[...].astype(F32) * conv).astype(BF16)


def forward(half, filters, k, v, q, rim, earlier):
    tokens, width = k.shape
    taps = rim.shape[0]
    groups = LANES * filters.shape[0] // width
    steps = width // LANES // 2
    at = lambda i: (0, i + half * steps)
    column = pl.BlockSpec((tokens, LANES), at)
    in_specs = [
        pl.BlockSpec((groups, taps), lambda i: (i + half * steps, 0)),
        column,
        column,
        column,
        pl.BlockSpec((taps, LANES), at),
    ]
    args = [filters, k, v, q, rim]
    aliases = {}
    if earlier is not None:
        in_specs += [pl.BlockSpec(memory_space=pl.ANY)] * 2
        args += list(earlier)
        aliases = {5: 0, 6: 1}
    return pl.pallas_call(
        functools.partial(forward_body, taps, groups),
        grid=(steps,),
        in_specs=in_specs,
        out_specs=[column, column, pl.BlockSpec((tokens, LANES), lambda i: (0, i))],
        out_shape=[
            jax.ShapeDtypeStruct((tokens, width), F32),
            jax.ShapeDtypeStruct((tokens, width), BF16),
            jax.ShapeDtypeStruct((tokens, width // 2), BF16),
        ],
        input_output_aliases=aliases,
        compiler_params=pltpu.CompilerParams(vmem_limit_bytes=16 * MIB),
        cost_estimate=LIGHT,
        name="conv_forward",
    )(*args)


def gate_body(place_ref, mine_ref, sib_ref, proj_ref, *refs):
    added, outs = refs[:-2], refs[-2:]
    rows = proj_ref.shape[0] // 8
    acc = None
    for dy in range(4):
        lhs = jnp.concatenate([mine_ref[dy], sib_ref[dy]], 1)
        rhs = jnp.concatenate(
            [
                proj_ref[pl.ds(pl.multiple_of(place_ref[2 * dy + i] * rows, rows), rows), :]
                for i in range(2)
            ],
            0,
        )
        term = jnp.dot(lhs, rhs, preferred_element_type=F32)
        acc = term if acc is None else acc + term
    second = pl.program_id(0) >= pl.num_programs(0) // 2
    if added:
        acc = acc + jnp.where(second, added[1][...], added[0][...]).astype(F32)
    acc = acc.astype(outs[0].dtype)

    @pl.when(jnp.logical_not(second))
    def _():
        outs[0][...] = acc

    @pl.when(second)
    def _():
        outs[1][...] = acc


def gate_parts(place, mine, sib, proj, wanted, dtype, *added):
    depth, width = proj.shape
    tokens = mine.shape[1] // 4
    tile = 256
    steps = width // 2 // tile
    (block0, half0), (block1, half1) = wanted
    choose = lambda i, first, second: jnp.where(i < steps, first, second)
    cot = pl.BlockSpec((4, tokens, depth // 8), lambda i, p: (0, choose(i, block0, block1), 0))
    pair = [
        pl.BlockSpec((tokens, tile), lambda i, p: (0, jnp.minimum(i, steps - 1))),
        pl.BlockSpec((tokens, tile), lambda i, p: (0, jnp.maximum(i - steps, 0))),
    ]
    spec = pltpu.PrefetchScalarGridSpec(
        num_scalar_prefetch=1,
        grid=(2 * steps,),
        in_specs=[
            cot,
            cot,
            pl.BlockSpec((depth, tile), lambda i, p: (0, i % steps + choose(i, half0, half1) * steps)),
        ]
        + pair[: len(added)],
        out_specs=pair,
    )
    return pl.pallas_call(
        gate_body,
        grid_spec=spec,
        out_shape=[jax.ShapeDtypeStruct((tokens, width // 2), dtype)] * 2,
        compiler_params=pltpu.CompilerParams(vmem_limit_bytes=16 * MIB),
        cost_estimate=LIGHT,
        name="grad_gate_parts",
    )(place, mine, sib, proj, *added)


def proj_body(place_ref, mine_ref, sib_ref, *refs):
    gated_refs, out_ref = refs[:-1], refs[-1]
    rows = mine_ref.shape[1]
    tokens, half = gated_refs[0].shape
    core = place_ref[0] % 2
    for h in range(2):
        acc = None
        for d in range(4):
            at = pl.ds(d * tokens, tokens)
            lhs = jnp.concatenate([mine_ref[at, :], sib_ref[at, :]], 1)
            term = lax.dot_general(
                lhs, gated_refs[2 * d + h][...], (((0,), (0,)), ((), ())), preferred_element_type=F32
            )
            acc = term if acc is None else acc + term
        acc = acc.astype(BF16)
        cols = pl.ds(h * half, half)
        out_ref[pl.ds(pl.multiple_of(core * rows, rows), rows), cols] = acc[:rows]
        out_ref[pl.ds(pl.multiple_of((1 - core) * rows, rows), rows), cols] = acc[rows:]


def proj_part(place, mine, sib, gated):
    rows = mine.shape[2]
    depth = 8 * rows
    tokens, half = gated[0].shape
    spec = pltpu.PrefetchScalarGridSpec(
        num_scalar_prefetch=1,
        grid=(4,),
        in_specs=[pl.BlockSpec((None, 4 * tokens, rows), lambda i, p: (i, 0, 0))] * 2
        + [pl.BlockSpec((tokens, half), lambda i, p: (0, 0))] * 8,
        out_specs=pl.BlockSpec((2 * rows, 2 * half), lambda i, p: (p[2 * i] // 2, 0)),
    )
    return pl.pallas_call(
        proj_body,
        grid_spec=spec,
        out_shape=jax.ShapeDtypeStruct((depth, 2 * half), BF16),
        compiler_params=pltpu.CompilerParams(vmem_limit_bytes=24 * MIB),
        cost_estimate=LIGHT,
        name="grad_proj_part",
    )(place, mine, sib, *gated)


def inner_body(*refs):
    own, from_left, from_right = refs[0:2], refs[2:4], refs[4:6]
    q_ref, conv_ref, query_ref, inner_ref = refs[6:]
    second = pl.program_id(0) >= pl.num_programs(0) // 2
    pick = lambda pair: jnp.where(second, pair[1][...], pair[0][...]).astype(F32)
    gate = pick(own) + pick(from_left) + pick(from_right)
    query_ref[...] = (gate * conv_ref[...]).astype(BF16)
    inner_ref[...] = (gate * q_ref[...].astype(F32)).astype(BF16)


def gate_gradients(own, from_left, from_right, q, conv):
    tokens, width = q.shape
    wide = 2 * LANES
    steps = width // wide
    column = pl.BlockSpec((tokens, wide), lambda i: (0, i))
    first = pl.BlockSpec((tokens, wide), lambda i: (0, jnp.minimum(i, steps // 2 - 1)))
    last = pl.BlockSpec((tokens, wide), lambda i: (0, jnp.maximum(i - steps // 2, 0)))
    return pl.pallas_call(
        inner_body,
        grid=(steps,),
        in_specs=[first, last] * 3 + [column, column],
        out_specs=[column, column],
        out_shape=[jax.ShapeDtypeStruct((tokens, width), BF16)] * 2,
        compiler_params=pltpu.CompilerParams(vmem_limit_bytes=16 * MIB),
        cost_estimate=LIGHT,
        name="gate_gradients",
    )(*own, *from_left, *from_right, q, conv)


def filter_body(taps, groups, inner_ref, mixed_ref, rim_ref, filter_ref):
    inner = inner_ref[...]
    window = jnp.concatenate([rim_ref[...], mixed_ref[...]], 0)
    blocks = inner.shape[0] // taps
    left = jnp.concatenate([inner[b * taps : (b + 1) * taps] for b in range(blocks)], 1)
    left = jnp.dot(anti_identity(taps), left, preferred_element_type=F32).astype(BF16)
    right = jnp.concatenate([window[b * taps : (b + 2) * taps] for b in range(blocks)], 1)
    lane_group = (lax.broadcasted_iota(jnp.int32, left.shape, 1) % LANES) // (LANES // groups)
    zero = jnp.zeros_like(left)
    stacked = jnp.concatenate([jnp.where(lane_group == g, left, zero) for g in range(groups)], 0)
    corr = lax.dot_general(stacked, right, (((1,), (1,)), ((), ())), preferred_element_type=F32)
    sums = [
        jnp.sum(
            pltpu.roll(corr[g * taps : (g + 1) * taps], 0, 1, stride=1, stride_axis=0),
            axis=0,
            keepdims=True,
        )[:, taps:]
        for g in range(groups)
    ]
    filter_ref[...] = jnp.concatenate(sums, 0)


def filter_part(inner, mixed, rim, group_count):
    tokens, width = inner.shape
    taps = rim.shape[0]
    groups = LANES * group_count // width
    column = pl.BlockSpec((tokens, LANES), lambda i: (0, i))
    return pl.pallas_call(
        functools.partial(filter_body, taps, groups),
        grid=(width // LANES,),
        in_specs=[column, column, pl.BlockSpec((taps, LANES), lambda i: (0, i))],
        out_specs=pl.BlockSpec((groups, taps), lambda i: (i, 0)),
        out_shape=jax.ShapeDtypeStruct((group_count, taps), F32),
        compiler_params=pltpu.CompilerParams(vmem_limit_bytes=16 * MIB),
        cost_estimate=LIGHT,
        name="filter_part",
    )(inner, mixed, rim)


def backward_body(taps, groups, filters_ref, inner_ref, ahead_ref, k_ref, v_ref, *refs):
    gk_ref, gv_ref = refs[-2:]
    window = jnp.concatenate([inner_ref[...], ahead_ref[...]], 0)
    grad = banded(group_tables(filters_ref[...], False), window, taps, groups)
    gk_ref[...] = (grad * v_ref[...].astype(F32)).astype(BF16)
    gv_ref[...] = (grad * k_ref[...].astype(F32)).astype(BF16)


def backward(half, filters, inner, ahead, k, v, earlier):
    tokens, width = k.shape
    taps = ahead.shape[0]
    groups = LANES * filters.shape[0] // width
    steps = width // LANES // 2
    at = lambda i: (0, i + half * steps)
    column = pl.BlockSpec((tokens, LANES), at)
    in_specs = [
        pl.BlockSpec((groups, taps), lambda i: (i + half * steps, 0)),
        column,
        pl.BlockSpec((taps, LANES), at),
        column,
        column,
    ]
    args = [filters, inner, ahead, k, v]
    aliases = {}
    if earlier is not None:
        in_specs += [pl.BlockSpec(memory_space=pl.ANY)] * 2
        args += list(earlier)
        aliases = {5: 0, 6: 1}
    return pl.pallas_call(
        functools.partial(backward_body, taps, groups),
        grid=(steps,),
        in_specs=in_specs,
        out_specs=[column, column],
        out_shape=[jax.ShapeDtypeStruct((tokens, width), BF16)] * 2,
        input_output_aliases=aliases,
        compiler_params=pltpu.CompilerParams(vmem_limit_bytes=16 * MIB),
        cost_estimate=LIGHT,
        name="conv_backward",
    )(*args)


def sum_over(value, axis, stride, *beside):
    count, me = lax.axis_size(axis) // stride, lax.axis_index(axis) // stride
    terms = [after(value, *beside)] + [send(value, axis, d * stride) for d in range(1, count)]
    total = None
    for source in range(count):
        term = terms[0]
        for d in range(1, count):
            term = jnp.where((me - source) % count == d, terms[d], term)
        total = term if total is None else total + term
    return total


def on_device(query_in, key_in, value_in, filters, proj_out, cotangent):
    tokens, width = query_in.shape
    group_count, taps = filters.shape
    half = width // 2
    x, y, c = (lax.axis_index(a) for a in ("x", "y", "c"))
    part = cotangent.shape[1] // 4

    proj = lax.all_gather(proj_out, "z", axis=0, tiled=True)

    last = product(key_in[tokens - taps :], value_in[tokens - taps :])
    rim = send_along_tokens(last, 1)
    base = after(x, last)
    own_cols = lambda d: lax.dynamic_slice_in_dim(cotangent, ((base + d) % 4) * part, part, 1)
    pieces = [own_cols(0), None, None, None]
    for d in (2, 1, 3):
        pieces[(-d) % 4] = send(own_cols(d), "x", d)
    conv, mixed, gated_a = forward(0, filters, key_in, value_in, query_in, rim, None)
    conv, mixed, gated_b = forward(1, filters, key_in, value_in, query_in, rim, (conv, mixed))
    column = after(jnp.concatenate(pieces, 0), gated_a)
    below, above = send(column, "y", 1), send(column, "y", -1)
    middle = column.shape[0] // 2
    far = send(below[:middle], "y", 1), send(above[middle:], "y", -1)
    left_a, right_a = send(gated_a, "x", 1), send(gated_a, "x", -1)
    right_b, left_b = send(gated_b, "x", -1), send(after(gated_b, left_a, right_a), "x", 1)
    far_a, far_b = send(left_a, "x", 1), send(right_b, "x", -1)
    gated = [gated_a, gated_b, right_a, right_b, far_a, far_b, left_a, left_b]

    far = after(far[0], left_a, right_b), far[1]
    mine = jnp.concatenate([column, above, *far, below], 0).reshape(4, 4 * tokens, part)
    sib = send(after(mine, right_a, left_b), "c", 1)
    place = jnp.stack([2 * ((y + dy) % 4) + (c if i == 0 else 1 - c) for dy in range(4) for i in range(2)])
    place = place.astype(jnp.int32)

    across = gate_parts(place, mine, sib, proj, ((2, 0), (2, 1)), BF16)
    far_a, far_b = send(across[0], "x", 1), send(across[1], "x", -1)
    proj = after(proj, *across, *gated[4:6])
    beside = gate_parts(place, mine, sib, proj, ((1, 1), (3, 0)), BF16)
    from_left_b, from_right_a = send(beside[0], "x", 1), send(beside[1], "x", -1)
    gated[0] = after(gated[0], *beside)
    proj_sums = proj_part(place, mine, sib, gated)

    joined = gate_parts(place, mine, sib, proj, ((1, 0), (3, 1)), BF16, far_a, far_b)
    from_left_a, from_right_b = send(joined[0], "x", 1), send(joined[1], "x", -1)
    proj_sums = after(proj_sums, from_left_b, from_right_a, joined[0])
    grad_proj = lax.psum_scatter(proj_sums, "z", scatter_dimension=0, tiled=True).astype(F32)
    own = gate_parts(place, mine, sib, proj, ((0, 0), (0, 1)), F32)
    from_left, from_right = (from_left_a, from_left_b), (from_right_a, from_right_b)

    first = [
        (
            (own[h][:taps] + from_left[h][:taps].astype(F32) + from_right[h][:taps].astype(F32))
            * query_in[:taps, h * half : (h + 1) * half].astype(F32)
        ).astype(BF16)
        for h in range(2)
    ]
    first = jnp.concatenate(first, 1)
    ahead = send_along_tokens(first, -1)
    grad_query, inner = gate_gradients(
        (after(own[0], first), own[1]), from_left, from_right, query_in, conv
    )
    sums = filter_part(inner, mixed, rim, group_count)
    grads = backward(0, filters, after(inner, sums), ahead, key_in, value_in, None)
    sums = sum_over(sums, "x", 1, *grads)
    grad_key, grad_value = backward(1, filters, after(inner, sums), ahead, key_in, value_in, grads)
    sums = sum_over(sums, "z", 2, grad_key)
    odd = lax.ppermute(sums, "z", [(i, i ^ 1) for i in range(lax.axis_size("z"))])
    grad_filter = jnp.flip(after(sums, grad_proj) + odd, 1)
    return grad_query, grad_key, grad_value, grad_filter, grad_proj


def solution(mesh):
    ctx, tp = mesh.devices.shape
    shape = (ctx // SIZE["x"], SIZE["x"], tp // SIZE["c"], SIZE["c"])
    fine = Mesh(mesh.devices.reshape(shape), AXES)
    spec, along = P(("z", "x"), ("y", "c")), P(("y", "c"), None)
    return jax.shard_map(
        on_device,
        mesh=fine,
        in_specs=(spec, spec, spec, along, spec, spec),
        out_specs=(spec, spec, spec, along, spec),
        check_vma=False,
    )
```

```python
import functools

import jax
import jax.numpy as jnp
from jax import lax
from jax.experimental import pallas as pl
from jax.experimental.pallas import tpu as pltpu
from jax.sharding import Mesh
from jax.sharding import PartitionSpec as P

F32, BF16 = jnp.float32, jnp.bfloat16
LANES = 128
AXES = ("z", "x", "y", "c")
SIZE = {"x": 4, "y": 4, "c": 2}
MIB = 1 << 20
LIGHT = pl.CostEstimate(flops=1 << 20, bytes_accessed=1 << 18, transcendentals=0)


def send(value, axis, by):
    count = lax.axis_size(axis)
    return lax.ppermute(value, axis, [(i, (i + by) % count) for i in range(count)])


def send_along_tokens(value, by):
    count = lax.axis_size("z") * lax.axis_size("x")
    pairs = [(i, i + by) for i in range(count) if 0 <= i + by < count]
    return lax.ppermute(value, ("z", "x"), pairs)


def after(value, *others):
    return lax.optimization_barrier((value, *others))[0]


def product(a, b):
    return (a.astype(F32) * b.astype(F32)).astype(BF16)


def anti_identity(size):
    at = sum(lax.broadcasted_iota(jnp.int32, (size, size), i) for i in range(2))
    return (at == size - 1).astype(F32).astype(BF16)


def group_tables(filters, reverse):
    taps = filters.shape[1]
    if reverse:
        filters = jnp.dot(filters, anti_identity(taps), preferred_element_type=F32)
    rows = jnp.concatenate([filters.astype(F32), jnp.zeros(filters.shape, F32)], 1)
    tables = [
        pltpu.roll(
            jnp.broadcast_to(rows[g : g + 1], (taps, 2 * taps)), int(reverse), 1, stride=1, stride_axis=0
        )
        for g in range(rows.shape[0])
    ]
    return jnp.concatenate(tables, 0).astype(BF16)


def banded(tables, window, taps, groups):
    lane_group = lax.broadcasted_iota(jnp.int32, (taps, LANES), 1) // (LANES // groups)
    blocks = window.shape[0] // taps - 1
    out = []
    for b in range(0, blocks, 2):
        pair = jnp.concatenate(
            [window[(b + i) * taps : (b + i + 2) * taps] for i in range(2)], 1
        )
        res = jnp.dot(tables, pair, preferred_element_type=F32)
        for i in range(2):
            cols = slice(i * LANES, (i + 1) * LANES)
            acc = res[:taps, cols]
            for g in range(1, groups):
                acc = jnp.where(lane_group == g, res[g * taps : (g + 1) * taps, cols], acc)
            out.append(acc)
    return jnp.concatenate(out, 0)


def forward_body(taps, groups, filters_ref, k_ref, v_ref, q_ref, rim_ref, *refs):
    conv_ref, mixed_ref, gated_ref = refs[-3:]
    mixed = product(k_ref[...], v_ref[...])
    window = jnp.concatenate([rim_ref[...], mixed], 0)
    conv = banded(group_tables(filters_ref[...], True), window, taps, groups)
    conv_ref[...] = conv
    mixed_ref[...] = mixed
    gated_ref[...] = (q_ref[...].astype(F32) * conv).astype(BF16)


def forward(half, filters, k, v, q, rim, earlier):
    tokens, width = k.shape
    taps = rim.shape[0]
    groups = LANES * filters.shape[0] // width
    steps = width // LANES // 2
    at = lambda i: (0, i + half * steps)
    column = pl.BlockSpec((tokens, LANES), at)
    in_specs = [
        pl.BlockSpec((groups, taps), lambda i: (i + half * steps, 0)),
        column,
        column,
        column,
        pl.BlockSpec((taps, LANES), at),
    ]
    args = [filters, k, v, q, rim]
    aliases = {}
    if earlier is not None:
        in_specs += [pl.BlockSpec(memory_space=pl.ANY)] * 2
        args += list(earlier)
        aliases = {5: 0, 6: 1}
    return pl.pallas_call(
        functools.partial(forward_body, taps, groups),
        grid=(steps,),
        in_specs=in_specs,
        out_specs=[column, column, pl.BlockSpec((tokens, LANES), lambda i: (0, i))],
        out_shape=[
            jax.ShapeDtypeStruct((tokens, width), F32),
            jax.ShapeDtypeStruct((tokens, width), BF16),
            jax.ShapeDtypeStruct((tokens, width // 2), BF16),
        ],
        input_output_aliases=aliases,
        compiler_params=pltpu.CompilerParams(vmem_limit_bytes=16 * MIB),
        cost_estimate=LIGHT,
        name="conv_forward",
    )(*args)


def join_body(*refs):
    pieces, out_ref = refs[:-2], refs[-1]
    rows = pieces[0].shape[0]
    for i, ref in enumerate(pieces):
        out_ref[i * rows : (i + 1) * rows] = ref[...]


def join(pieces, later_than):
    rows, width = pieces[0].shape
    return pl.pallas_call(
        join_body,
        in_specs=[pl.BlockSpec(memory_space=pltpu.VMEM)] * len(pieces) + [pl.BlockSpec(memory_space=pl.ANY)],
        out_specs=pl.BlockSpec(memory_space=pltpu.VMEM),
        out_shape=jax.ShapeDtypeStruct((len(pieces) * rows, width), pieces[0].dtype),
        compiler_params=pltpu.CompilerParams(vmem_limit_bytes=4 * MIB),
        cost_estimate=LIGHT,
        name="join",
    )(*pieces, later_than)


def gate_body(place_ref, mine_ref, sib_ref, proj_ref, *refs):
    added, outs = refs[:-2], refs[-2:]
    rows = proj_ref.shape[0] // 8
    acc = None
    for dy in range(4):
        lhs = jnp.concatenate([mine_ref[dy], sib_ref[dy]], 1)
        rhs = jnp.concatenate(
            [
                proj_ref[pl.ds(pl.multiple_of(place_ref[2 * dy + i] * rows, rows), rows), :]
                for i in range(2)
            ],
            0,
        )
        term = jnp.dot(lhs, rhs, preferred_element_type=F32)
        acc = term if acc is None else acc + term
    second = pl.program_id(0) >= pl.num_programs(0) // 2
    if added:
        acc = acc + jnp.where(second, added[1][...], added[0][...]).astype(F32)
    acc = acc.astype(outs[0].dtype)

    @pl.when(jnp.logical_not(second))
    def _():
        outs[0][...] = acc

    @pl.when(second)
    def _():
        outs[1][...] = acc


def gate_parts(place, mine, sib, proj, wanted, dtype, *added):
    depth, width = proj.shape
    tokens = mine.shape[1] // 4
    tile = 256
    steps = width // 2 // tile
    (block0, half0), (block1, half1) = wanted
    choose = lambda i, first, second: jnp.where(i < steps, first, second)
    cot = pl.BlockSpec((4, tokens, depth // 8), lambda i, p: (0, choose(i, block0, block1), 0))
    pair = [
        pl.BlockSpec((tokens, tile), lambda i, p: (0, jnp.minimum(i, steps - 1))),
        pl.BlockSpec((tokens, tile), lambda i, p: (0, jnp.maximum(i - steps, 0))),
    ]
    spec = pltpu.PrefetchScalarGridSpec(
        num_scalar_prefetch=1,
        grid=(2 * steps,),
        in_specs=[
            cot,
            cot,
            pl.BlockSpec((depth, tile), lambda i, p: (0, i % steps + choose(i, half0, half1) * steps)),
        ]
        + pair[: len(added)],
        out_specs=pair,
    )
    return pl.pallas_call(
        gate_body,
        grid_spec=spec,
        out_shape=[jax.ShapeDtypeStruct((tokens, width // 2), dtype)] * 2,
        compiler_params=pltpu.CompilerParams(vmem_limit_bytes=(16 if dtype == F32 else 60) * MIB),
        cost_estimate=LIGHT,
        name="grad_gate_parts",
    )(place, mine, sib, proj, *added)


def proj_body(place_ref, mine_ref, sib_ref, *refs):
    gated_refs, out_ref = refs[:-1], refs[-1]
    rows = mine_ref.shape[1]
    tokens, half = gated_refs[0].shape
    core = place_ref[0] % 2
    for h in range(2):
        acc = None
        for d in range(4):
            at = pl.ds(d * tokens, tokens)
            lhs = jnp.concatenate([mine_ref[at, :], sib_ref[at, :]], 1)
            term = lax.dot_general(
                lhs, gated_refs[2 * d + h][...], (((0,), (0,)), ((), ())), preferred_element_type=F32
            )
            acc = term if acc is None else acc + term
        acc = acc.astype(BF16)
        cols = pl.ds(h * half, half)
        out_ref[pl.ds(pl.multiple_of(core * rows, rows), rows), cols] = acc[:rows]
        out_ref[pl.ds(pl.multiple_of((1 - core) * rows, rows), rows), cols] = acc[rows:]


def proj_part(place, mine, sib, gated):
    rows = mine.shape[2]
    depth = 8 * rows
    tokens, half = gated[0].shape
    spec = pltpu.PrefetchScalarGridSpec(
        num_scalar_prefetch=1,
        grid=(4,),
        in_specs=[pl.BlockSpec((None, 4 * tokens, rows), lambda i, p: (i, 0, 0))] * 2
        + [pl.BlockSpec((tokens, half), lambda i, p: (0, 0))] * 8,
        out_specs=pl.BlockSpec((2 * rows, 2 * half), lambda i, p: (p[2 * i] // 2, 0)),
    )
    return pl.pallas_call(
        proj_body,
        grid_spec=spec,
        out_shape=jax.ShapeDtypeStruct((depth, 2 * half), BF16),
        compiler_params=pltpu.CompilerParams(vmem_limit_bytes=60 * MIB),
        cost_estimate=LIGHT,
        name="grad_proj_part",
    )(place, mine, sib, *gated)


def inner_body(*refs):
    own, from_left, from_right = refs[0:2], refs[2:4], refs[4:6]
    q_ref, conv_ref, query_ref, inner_ref, first_ref = refs[6:]
    second = pl.program_id(0) >= pl.num_programs(0) // 2
    pick = lambda pair: jnp.where(second, pair[1][...], pair[0][...]).astype(F32)
    gate = pick(own) + pick(from_left) + pick(from_right)
    query_ref[...] = (gate * conv_ref[...]).astype(BF16)
    inner = (gate * q_ref[...].astype(F32)).astype(BF16)
    inner_ref[...] = inner
    first_ref[...] = inner[: first_ref.shape[0]]


def gate_gradients(own, from_left, from_right, q, conv, taps):
    tokens, width = q.shape
    wide = 2 * LANES
    steps = width // wide
    column = pl.BlockSpec((tokens, wide), lambda i: (0, i))
    first = pl.BlockSpec((tokens, wide), lambda i: (0, jnp.minimum(i, steps // 2 - 1)))
    last = pl.BlockSpec((tokens, wide), lambda i: (0, jnp.maximum(i - steps // 2, 0)))
    return pl.pallas_call(
        inner_body,
        grid=(steps,),
        in_specs=[first, last] * 3 + [column, column],
        out_specs=[column, column, pl.BlockSpec((taps, wide), lambda i: (0, i))],
        out_shape=[jax.ShapeDtypeStruct((n, width), BF16) for n in (tokens, tokens, taps)],
        compiler_params=pltpu.CompilerParams(vmem_limit_bytes=16 * MIB),
        cost_estimate=LIGHT,
        name="gate_gradients",
    )(*own, *from_left, *from_right, q, conv)


def filter_body(taps, groups, inner_ref, mixed_ref, rim_ref, filter_ref):
    inner = inner_ref[...]
    window = jnp.concatenate([rim_ref[...], mixed_ref[...]], 0)
    blocks = inner.shape[0] // taps
    left = jnp.concatenate([inner[b * taps : (b + 1) * taps] for b in range(blocks)], 1)
    left = jnp.dot(anti_identity(taps), left, preferred_element_type=F32).astype(BF16)
    right = jnp.concatenate([window[b * taps : (b + 2) * taps] for b in range(blocks)], 1)
    lane_group = (lax.broadcasted_iota(jnp.int32, left.shape, 1) % LANES) // (LANES // groups)
    zero = jnp.zeros_like(left)
    stacked = jnp.concatenate([jnp.where(lane_group == g, left, zero) for g in range(groups)], 0)
    corr = lax.dot_general(stacked, right, (((1,), (1,)), ((), ())), preferred_element_type=F32)
    sums = [
        jnp.sum(
            pltpu.roll(corr[g * taps : (g + 1) * taps], 0, 1, stride=1, stride_axis=0),
            axis=0,
            keepdims=True,
        )[:, taps:]
        for g in range(groups)
    ]
    filter_ref[...] = jnp.concatenate(sums, 0)


def filter_part(inner, mixed, rim, group_count):
    tokens, width = inner.shape
    taps = rim.shape[0]
    groups = LANES * group_count // width
    column = pl.BlockSpec((tokens, LANES), lambda i: (0, i))
    return pl.pallas_call(
        functools.partial(filter_body, taps, groups),
        grid=(width // LANES,),
        in_specs=[column, column, pl.BlockSpec((taps, LANES), lambda i: (0, i))],
        out_specs=pl.BlockSpec((groups, taps), lambda i: (i, 0)),
        out_shape=jax.ShapeDtypeStruct((group_count, taps), F32),
        compiler_params=pltpu.CompilerParams(vmem_limit_bytes=16 * MIB),
        cost_estimate=LIGHT,
        name="filter_part",
    )(inner, mixed, rim)


def backward_body(taps, groups, filters_ref, inner_ref, ahead_ref, k_ref, v_ref, *refs):
    gk_ref, gv_ref = refs[-2:]
    window = jnp.concatenate([inner_ref[...], ahead_ref[...]], 0)
    grad = banded(group_tables(filters_ref[...], False), window, taps, groups)
    gk_ref[...] = (grad * v_ref[...].astype(F32)).astype(BF16)
    gv_ref[...] = (grad * k_ref[...].astype(F32)).astype(BF16)


def backward(half, filters, inner, ahead, k, v, earlier):
    tokens, width = k.shape
    taps = ahead.shape[0]
    groups = LANES * filters.shape[0] // width
    steps = width // LANES // 2
    at = lambda i: (0, i + half * steps)
    column = pl.BlockSpec((tokens, LANES), at)
    in_specs = [
        pl.BlockSpec((groups, taps), lambda i: (i + half * steps, 0)),
        column,
        pl.BlockSpec((taps, LANES), at),
        column,
        column,
    ]
    args = [filters, inner, ahead, k, v]
    aliases = {}
    if earlier is not None:
        in_specs += [pl.BlockSpec(memory_space=pl.ANY)] * 2
        args += list(earlier)
        aliases = {5: 0, 6: 1}
    return pl.pallas_call(
        functools.partial(backward_body, taps, groups),
        grid=(steps,),
        in_specs=in_specs,
        out_specs=[column, column],
        out_shape=[jax.ShapeDtypeStruct((tokens, width), BF16)] * 2,
        input_output_aliases=aliases,
        compiler_params=pltpu.CompilerParams(vmem_limit_bytes=16 * MIB),
        cost_estimate=LIGHT,
        name="conv_backward",
    )(*args)


def sum_over(value, axis, stride, *beside):
    count, me = lax.axis_size(axis) // stride, lax.axis_index(axis) // stride
    terms = [after(value, *beside)] + [send(value, axis, d * stride) for d in range(1, count)]
    total = None
    for source in range(count):
        term = terms[0]
        for d in range(1, count):
            term = jnp.where((me - source) % count == d, terms[d], term)
        total = term if total is None else total + term
    return total


def on_device(query_in, key_in, value_in, filters, proj_out, cotangent):
    tokens, width = query_in.shape
    group_count, taps = filters.shape
    half = width // 2
    x, y, c = (lax.axis_index(a) for a in ("x", "y", "c"))
    part = cotangent.shape[1] // 4

    proj = lax.all_gather(proj_out, "z", axis=0, tiled=True)

    last = product(key_in[tokens - taps :], value_in[tokens - taps :])
    rim = send_along_tokens(last, 1)
    base = after(x, last)
    own_cols = lambda d: lax.dynamic_slice_in_dim(cotangent, ((base + d) % 4) * part, part, 1)
    pieces = [own_cols(0), None, None, None]
    for d in (2, 1, 3):
        pieces[(-d) % 4] = send(own_cols(d), "x", d)
    conv, mixed, gated_a = forward(0, filters, key_in, value_in, query_in, rim, None)
    conv, mixed, gated_b = forward(1, filters, key_in, value_in, query_in, rim, (conv, mixed))
    column = join(pieces, gated_b)
    below, above = send(column, "y", 1), send(column, "y", -1)
    middle = column.shape[0] // 2
    far = send(below[:middle], "y", 1), send(above[middle:], "y", -1)
    left_a, right_a = send(gated_a, "x", 1), send(gated_a, "x", -1)
    right_b, left_b = send(gated_b, "x", -1), send(after(gated_b, left_a, right_a), "x", 1)
    far_a, far_b = send(left_a, "x", 1), send(right_b, "x", -1)
    gated = [gated_a, gated_b, right_a, right_b, far_a, far_b, left_a, left_b]

    far = after(far[0], left_a, right_b), far[1]
    mine = jnp.concatenate([column, above, *far, below], 0).reshape(4, 4 * tokens, part)
    sib = send(after(mine, right_a, left_b), "c", 1)
    place = jnp.stack([2 * ((y + dy) % 4) + (c if i == 0 else 1 - c) for dy in range(4) for i in range(2)])
    place = place.astype(jnp.int32)

    across = gate_parts(place, mine, sib, proj, ((2, 0), (2, 1)), BF16)
    far_a, far_b = send(across[0], "x", 1), send(across[1], "x", -1)
    proj = after(proj, *across, *gated[4:6])
    beside = gate_parts(place, mine, sib, proj, ((1, 1), (3, 0)), BF16)
    from_left_b, from_right_a = send(beside[0], "x", 1), send(beside[1], "x", -1)
    gated[0] = after(gated[0], *beside)
    proj_sums = proj_part(place, mine, sib, gated)

    joined = gate_parts(place, mine, sib, proj, ((1, 0), (3, 1)), BF16, far_a, far_b)
    from_left_a, from_right_b = send(joined[0], "x", 1), send(joined[1], "x", -1)
    proj_sums = after(proj_sums, from_left_b, from_right_a, joined[0])
    grad_proj = lax.psum_scatter(proj_sums, "z", scatter_dimension=0, tiled=True).astype(F32)
    own = gate_parts(place, mine, sib, proj, ((0, 0), (0, 1)), F32)
    from_left, from_right = (from_left_a, from_left_b), (from_right_a, from_right_b)

    grad_query, inner, first = gate_gradients(own, from_left, from_right, query_in, conv, taps)
    ahead = send_along_tokens(first, -1)
    sums = filter_part(inner, mixed, rim, group_count)
    grads = backward(0, filters, after(inner, sums), ahead, key_in, value_in, None)
    sums = sum_over(sums, "x", 1, *grads)
    grad_key, grad_value = backward(1, filters, after(inner, sums), ahead, key_in, value_in, grads)
    sums = sum_over(sums, "z", 2, grad_key)
    odd = lax.ppermute(sums, "z", [(i, i ^ 1) for i in range(lax.axis_size("z"))])
    grad_filter = jnp.flip(after(sums, grad_proj) + odd, 1)
    return grad_query, grad_key, grad_value, grad_filter, grad_proj


def solution(mesh):
    ctx, tp = mesh.devices.shape
    shape = (ctx // SIZE["x"], SIZE["x"], tp // SIZE["c"], SIZE["c"])
    fine = Mesh(mesh.devices.reshape(shape), AXES)
    spec, along = P(("z", "x"), ("y", "c")), P(("y", "c"), None)
    return jax.shard_map(
        on_device,
        mesh=fine,
        in_specs=(spec, spec, spec, along, spec, spec),
        out_specs=(spec, spec, spec, along, spec),
        check_vma=False,
    )
```

```python
import functools

import jax
import jax.numpy as jnp
from jax import lax
from jax.experimental import pallas as pl
from jax.experimental.pallas import tpu as pltpu
from jax.sharding import Mesh
from jax.sharding import PartitionSpec as P

F32, BF16 = jnp.float32, jnp.bfloat16
LANES = 128
AXES = ("z", "x", "y", "c")
SIZE = {"x": 4, "y": 4, "c": 2}
MIB = 1 << 20
LIGHT = pl.CostEstimate(flops=1 << 20, bytes_accessed=1 << 18, transcendentals=0)


def send(value, axis, by):
    count = lax.axis_size(axis)
    return lax.ppermute(value, axis, [(i, (i + by) % count) for i in range(count)])


def send_along_tokens(value, by):
    count = lax.axis_size("z") * lax.axis_size("x")
    pairs = [(i, i + by) for i in range(count) if 0 <= i + by < count]
    return lax.ppermute(value, ("z", "x"), pairs)


def after(value, *others):
    return lax.optimization_barrier((value, *others))[0]


def product(a, b):
    return (a.astype(F32) * b.astype(F32)).astype(BF16)


def anti_identity(size):
    at = sum(lax.broadcasted_iota(jnp.int32, (size, size), i) for i in range(2))
    return (at == size - 1).astype(F32).astype(BF16)


def group_tables(filters, reverse):
    taps = filters.shape[1]
    if reverse:
        filters = jnp.dot(filters, anti_identity(taps), preferred_element_type=F32)
    rows = jnp.concatenate([filters.astype(F32), jnp.zeros(filters.shape, F32)], 1)
    tables = [
        pltpu.roll(
            jnp.broadcast_to(rows[g : g + 1], (taps, 2 * taps)), int(reverse), 1, stride=1, stride_axis=0
        )
        for g in range(rows.shape[0])
    ]
    return jnp.concatenate(tables, 0).astype(BF16)


def banded(tables, window, taps, groups):
    lane_group = lax.broadcasted_iota(jnp.int32, (taps, LANES), 1) // (LANES // groups)
    blocks = window.shape[0] // taps - 1
    out = []
    for b in range(0, blocks, 2):
        pair = jnp.concatenate(
            [window[(b + i) * taps : (b + i + 2) * taps] for i in range(2)], 1
        )
        res = jnp.dot(tables, pair, preferred_element_type=F32)
        for i in range(2):
            cols = slice(i * LANES, (i + 1) * LANES)
            acc = res[:taps, cols]
            for g in range(1, groups):
                acc = jnp.where(lane_group == g, res[g * taps : (g + 1) * taps, cols], acc)
            out.append(acc)
    return jnp.concatenate(out, 0)


def forward_body(taps, groups, filters_ref, k_ref, v_ref, q_ref, rim_ref, *refs):
    conv_ref, mixed_ref, gated_ref = refs[-3:]
    mixed = product(k_ref[...], v_ref[...])
    window = jnp.concatenate([rim_ref[...], mixed], 0)
    conv = banded(group_tables(filters_ref[...], True), window, taps, groups)
    conv_ref[...] = conv
    mixed_ref[...] = mixed
    gated_ref[...] = (q_ref[...].astype(F32) * conv).astype(BF16)


def forward(half, filters, k, v, q, rim, earlier):
    tokens, width = k.shape
    taps = rim.shape[0]
    groups = LANES * filters.shape[0] // width
    steps = width // LANES // 2
    at = lambda i: (0, i + half * steps)
    column = pl.BlockSpec((tokens, LANES), at)
    in_specs = [
        pl.BlockSpec((groups, taps), lambda i: (i + half * steps, 0)),
        column,
        column,
        column,
        pl.BlockSpec((taps, LANES), at),
    ]
    args = [filters, k, v, q, rim]
    aliases = {}
    if earlier is not None:
        in_specs += [pl.BlockSpec(memory_space=pl.ANY)] * 2
        args += list(earlier)
        aliases = {5: 0, 6: 1}
    return pl.pallas_call(
        functools.partial(forward_body, taps, groups),
        grid=(steps,),
        in_specs=in_specs,
        out_specs=[column, column, pl.BlockSpec((tokens, LANES), lambda i: (0, i))],
        out_shape=[
            jax.ShapeDtypeStruct((tokens, width), F32),
            jax.ShapeDtypeStruct((tokens, width), BF16),
            jax.ShapeDtypeStruct((tokens, width // 2), BF16),
        ],
        input_output_aliases=aliases,
        compiler_params=pltpu.CompilerParams(vmem_limit_bytes=16 * MIB),
        cost_estimate=LIGHT,
        name="conv_forward",
    )(*args)


def join_body(*refs):
    pieces, out_ref = refs[:-2], refs[-1]
    rows = pieces[0].shape[0]
    for i, ref in enumerate(pieces):
        out_ref[i * rows : (i + 1) * rows] = ref[...]


def join(pieces, later_than):
    rows, width = pieces[0].shape
    return pl.pallas_call(
        join_body,
        in_specs=[pl.BlockSpec(memory_space=pltpu.VMEM)] * len(pieces) + [pl.BlockSpec(memory_space=pl.ANY)],
        out_specs=pl.BlockSpec(memory_space=pltpu.VMEM),
        out_shape=jax.ShapeDtypeStruct((len(pieces) * rows, width), pieces[0].dtype),
        compiler_params=pltpu.CompilerParams(vmem_limit_bytes=4 * MIB),
        cost_estimate=LIGHT,
        name="join",
    )(*pieces, later_than)


def gate_body(wanted, place_ref, mine_ref, sib_ref, proj_ref, *refs):
    added, outs = refs[:-2], refs[-2:]
    rows = proj_ref.shape[0] // 8
    tokens, half = outs[0].shape
    tile = 256
    for n, (block, side) in enumerate(wanted):
        at = pl.ds(block * tokens, tokens)
        lhs = [jnp.concatenate([mine_ref[dy, at], sib_ref[dy, at]], 1) for dy in range(4)]
        for start in range(0, half, tile):
            cols = pl.ds(side * half + start, tile)
            acc = None
            for dy in range(4):
                rhs = jnp.concatenate(
                    [
                        proj_ref[pl.ds(pl.multiple_of(place_ref[2 * dy + i] * rows, rows), rows), cols]
                        for i in range(2)
                    ],
                    0,
                )
                term = jnp.dot(lhs[dy], rhs, preferred_element_type=F32)
                acc = term if acc is None else acc + term
            here = pl.ds(start, tile)
            if added:
                acc = acc + added[n][:, here].astype(F32)
            outs[n][:, here] = acc.astype(outs[n].dtype)


RESIDENT = pl.BlockSpec(memory_space=pltpu.VMEM)


def gate_parts(place, mine, sib, proj, wanted, dtype, *added):
    width = proj.shape[1]
    tokens = mine.shape[1] // 4
    return pl.pallas_call(
        functools.partial(gate_body, wanted),
        in_specs=[pl.BlockSpec(memory_space=pltpu.SMEM)] + [RESIDENT] * (3 + len(added)),
        out_specs=[RESIDENT] * 2,
        out_shape=[jax.ShapeDtypeStruct((tokens, width // 2), dtype)] * 2,
        compiler_params=pltpu.CompilerParams(vmem_limit_bytes=14 * MIB),
        cost_estimate=LIGHT,
        name="grad_gate_parts",
    )(place, mine, sib, proj, *added)


def proj_body(place_ref, mine_ref, sib_ref, *refs):
    gated_refs, out_ref = refs[:-1], refs[-1]
    rows = mine_ref.shape[2]
    tokens, half = gated_refs[0].shape
    for dy in range(4):
        lhs = [
            jnp.concatenate([mine_ref[dy, at], sib_ref[dy, at]], 1)
            for at in (pl.ds(d * tokens, tokens) for d in range(4))
        ]
        for h in range(2):
            acc = None
            for d in range(4):
                term = lax.dot_general(
                    lhs[d],
                    gated_refs[2 * d + h][...],
                    (((0,), (0,)), ((), ())),
                    preferred_element_type=F32,
                )
                acc = term if acc is None else acc + term
            acc = acc.astype(BF16)
            cols = pl.ds(h * half, half)
            for i in range(2):
                to = pl.ds(pl.multiple_of(place_ref[2 * dy + i] * rows, rows), rows)
                out_ref[to, cols] = acc[i * rows : (i + 1) * rows]


def proj_part(place, mine, sib, gated):
    half = gated[0].shape[1]
    return pl.pallas_call(
        proj_body,
        in_specs=[pl.BlockSpec(memory_space=pltpu.SMEM)] + [RESIDENT] * 10,
        out_specs=RESIDENT,
        out_shape=jax.ShapeDtypeStruct((8 * mine.shape[2], 2 * half), BF16),
        compiler_params=pltpu.CompilerParams(vmem_limit_bytes=14 * MIB),
        cost_estimate=LIGHT,
        name="grad_proj_part",
    )(place, mine, sib, *gated)


def inner_body(*refs):
    own, from_left, from_right = refs[0:2], refs[2:4], refs[4:6]
    q_ref, conv_ref, query_ref, inner_ref, first_ref = refs[6:]
    second = pl.program_id(0) >= pl.num_programs(0) // 2
    pick = lambda pair: jnp.where(second, pair[1][...], pair[0][...]).astype(F32)
    gate = pick(own) + pick(from_left) + pick(from_right)
    query_ref[...] = (gate * conv_ref[...]).astype(BF16)
    inner = (gate * q_ref[...].astype(F32)).astype(BF16)
    inner_ref[...] = inner
    first_ref[...] = inner[: first_ref.shape[0]]


def gate_gradients(own, from_left, from_right, q, conv, taps):
    tokens, width = q.shape
    wide = 2 * LANES
    steps = width // wide
    column = pl.BlockSpec((tokens, wide), lambda i: (0, i))
    first = pl.BlockSpec((tokens, wide), lambda i: (0, jnp.minimum(i, steps // 2 - 1)))
    last = pl.BlockSpec((tokens, wide), lambda i: (0, jnp.maximum(i - steps // 2, 0)))
    return pl.pallas_call(
        inner_body,
        grid=(steps,),
        in_specs=[first, last] * 3 + [column, column],
        out_specs=[column, column, pl.BlockSpec((taps, wide), lambda i: (0, i))],
        out_shape=[jax.ShapeDtypeStruct((n, width), BF16) for n in (tokens, tokens, taps)],
        compiler_params=pltpu.CompilerParams(vmem_limit_bytes=16 * MIB),
        cost_estimate=LIGHT,
        name="gate_gradients",
    )(*own, *from_left, *from_right, q, conv)


def filter_body(taps, groups, inner_ref, mixed_ref, rim_ref, filter_ref):
    inner = inner_ref[...]
    window = jnp.concatenate([rim_ref[...], mixed_ref[...]], 0)
    blocks = inner.shape[0] // taps
    left = jnp.concatenate([inner[b * taps : (b + 1) * taps] for b in range(blocks)], 1)
    left = jnp.dot(anti_identity(taps), left, preferred_element_type=F32).astype(BF16)
    right = jnp.concatenate([window[b * taps : (b + 2) * taps] for b in range(blocks)], 1)
    lane_group = (lax.broadcasted_iota(jnp.int32, left.shape, 1) % LANES) // (LANES // groups)
    zero = jnp.zeros_like(left)
    stacked = jnp.concatenate([jnp.where(lane_group == g, left, zero) for g in range(groups)], 0)
    corr = lax.dot_general(stacked, right, (((1,), (1,)), ((), ())), preferred_element_type=F32)
    sums = [
        jnp.sum(
            pltpu.roll(corr[g * taps : (g + 1) * taps], 0, 1, stride=1, stride_axis=0),
            axis=0,
            keepdims=True,
        )[:, taps:]
        for g in range(groups)
    ]
    filter_ref[...] = jnp.concatenate(sums, 0)


def filter_part(inner, mixed, rim, group_count):
    tokens, width = inner.shape
    taps = rim.shape[0]
    groups = LANES * group_count // width
    column = pl.BlockSpec((tokens, LANES), lambda i: (0, i))
    return pl.pallas_call(
        functools.partial(filter_body, taps, groups),
        grid=(width // LANES,),
        in_specs=[column, column, pl.BlockSpec((taps, LANES), lambda i: (0, i))],
        out_specs=pl.BlockSpec((groups, taps), lambda i: (i, 0)),
        out_shape=jax.ShapeDtypeStruct((group_count, taps), F32),
        compiler_params=pltpu.CompilerParams(vmem_limit_bytes=16 * MIB),
        cost_estimate=LIGHT,
        name="filter_part",
    )(inner, mixed, rim)


def backward_body(taps, groups, filters_ref, inner_ref, ahead_ref, k_ref, v_ref, *refs):
    gk_ref, gv_ref = refs[-2:]
    window = jnp.concatenate([inner_ref[...], ahead_ref[...]], 0)
    grad = banded(group_tables(filters_ref[...], False), window, taps, groups)
    gk_ref[...] = (grad * v_ref[...].astype(F32)).astype(BF16)
    gv_ref[...] = (grad * k_ref[...].astype(F32)).astype(BF16)


def backward(half, filters, inner, ahead, k, v, earlier):
    tokens, width = k.shape
    taps = ahead.shape[0]
    groups = LANES * filters.shape[0] // width
    steps = width // LANES // 2
    at = lambda i: (0, i + half * steps)
    column = pl.BlockSpec((tokens, LANES), at)
    in_specs = [
        pl.BlockSpec((groups, taps), lambda i: (i + half * steps, 0)),
        column,
        pl.BlockSpec((taps, LANES), at),
        column,
        column,
    ]
    args = [filters, inner, ahead, k, v]
    aliases = {}
    if earlier is not None:
        in_specs += [pl.BlockSpec(memory_space=pl.ANY)] * 2
        args += list(earlier)
        aliases = {5: 0, 6: 1}
    return pl.pallas_call(
        functools.partial(backward_body, taps, groups),
        grid=(steps,),
        in_specs=in_specs,
        out_specs=[column, column],
        out_shape=[jax.ShapeDtypeStruct((tokens, width), BF16)] * 2,
        input_output_aliases=aliases,
        compiler_params=pltpu.CompilerParams(vmem_limit_bytes=16 * MIB),
        cost_estimate=LIGHT,
        name="conv_backward",
    )(*args)


def sum_over(value, axis, stride, *beside):
    count, me = lax.axis_size(axis) // stride, lax.axis_index(axis) // stride
    terms = [after(value, *beside)] + [send(value, axis, d * stride) for d in range(1, count)]
    total = None
    for source in range(count):
        term = terms[0]
        for d in range(1, count):
            term = jnp.where((me - source) % count == d, terms[d], term)
        total = term if total is None else total + term
    return total


def on_device(query_in, key_in, value_in, filters, proj_out, cotangent):
    tokens, width = query_in.shape
    group_count, taps = filters.shape
    half = width // 2
    x, y, c = (lax.axis_index(a) for a in ("x", "y", "c"))
    part = cotangent.shape[1] // 4

    proj = lax.all_gather(proj_out, "z", axis=0, tiled=True)

    last = product(key_in[tokens - taps :], value_in[tokens - taps :])
    rim = send_along_tokens(last, 1)
    base = after(x, last)
    own_cols = lambda d: lax.dynamic_slice_in_dim(cotangent, ((base + d) % 4) * part, part, 1)
    pieces = [own_cols(0), None, None, None]
    for d in (2, 1, 3):
        pieces[(-d) % 4] = send(own_cols(d), "x", d)
    conv, mixed, gated_a = forward(0, filters, key_in, value_in, query_in, rim, None)
    conv, mixed, gated_b = forward(1, filters, key_in, value_in, query_in, rim, (conv, mixed))
    column = join(pieces, gated_b)
    below, above = send(column, "y", 1), send(column, "y", -1)
    middle = column.shape[0] // 2
    far = send(below[:middle], "y", 1), send(above[middle:], "y", -1)
    left_a, right_a = send(gated_a, "x", 1), send(gated_a, "x", -1)
    right_b, left_b = send(gated_b, "x", -1), send(after(gated_b, left_a, right_a), "x", 1)
    far_a, far_b = send(left_a, "x", 1), send(right_b, "x", -1)
    gated = [gated_a, gated_b, right_a, right_b, far_a, far_b, left_a, left_b]

    far = after(far[0], left_a, right_b), far[1]
    mine = jnp.concatenate([column, above, *far, below], 0).reshape(4, 4 * tokens, part)
    sib = send(after(mine, right_a, left_b), "c", 1)
    place = jnp.stack([2 * ((y + dy) % 4) + (c if i == 0 else 1 - c) for dy in range(4) for i in range(2)])
    place = place.astype(jnp.int32)

    across = gate_parts(place, mine, sib, proj, ((2, 0), (2, 1)), BF16)
    far_a, far_b = send(across[0], "x", 1), send(across[1], "x", -1)
    proj = after(proj, *across)
    beside = gate_parts(place, mine, sib, proj, ((1, 1), (3, 0)), BF16)
    from_left_b, from_right_a = send(beside[0], "x", 1), send(beside[1], "x", -1)
    gated[0] = after(gated[0], *beside)
    proj_sums = proj_part(place, mine, sib, gated)

    joined = gate_parts(place, mine, sib, proj, ((1, 0), (3, 1)), BF16, far_a, far_b)
    from_left_a, from_right_b = send(joined[0], "x", 1), send(joined[1], "x", -1)
    proj_sums = after(proj_sums, from_left_b, from_right_a, joined[0])
    grad_proj = lax.psum_scatter(proj_sums, "z", scatter_dimension=0, tiled=True).astype(F32)
    own = gate_parts(place, mine, sib, proj, ((0, 0), (0, 1)), F32)
    from_left, from_right = (from_left_a, from_left_b), (from_right_a, from_right_b)

    grad_query, inner, first = gate_gradients(own, from_left, from_right, query_in, conv, taps)
    ahead = send_along_tokens(first, -1)
    sums = filter_part(inner, mixed, rim, group_count)
    grads = backward(0, filters, after(inner, sums), ahead, key_in, value_in, None)
    sums = sum_over(sums, "x", 1, *grads)
    grad_key, grad_value = backward(1, filters, after(inner, sums), ahead, key_in, value_in, grads)
    sums = sum_over(sums, "z", 2, grad_key)
    odd = lax.ppermute(sums, "z", [(i, i ^ 1) for i in range(lax.axis_size("z"))])
    grad_filter = jnp.flip(after(sums, grad_proj) + odd, 1)
    return grad_query, grad_key, grad_value, grad_filter, grad_proj


def solution(mesh):
    ctx, tp = mesh.devices.shape
    shape = (ctx // SIZE["x"], SIZE["x"], tp // SIZE["c"], SIZE["c"])
    fine = Mesh(mesh.devices.reshape(shape), AXES)
    spec, along = P(("z", "x"), ("y", "c")), P(("y", "c"), None)
    return jax.shard_map(
        on_device,
        mesh=fine,
        in_specs=(spec, spec, spec, along, spec, spec),
        out_specs=(spec, spec, spec, along, spec),
        check_vma=False,
    )
```

```python
import functools

import jax
import jax.numpy as jnp
from jax import lax
from jax.experimental import pallas as pl
from jax.experimental.pallas import tpu as pltpu
from jax.sharding import Mesh
from jax.sharding import PartitionSpec as P

F32, BF16 = jnp.float32, jnp.bfloat16
LANES = 128
AXES = ("z", "x", "y", "c")
SIZE = {"x": 4, "y": 4, "c": 2}
MIB = 1 << 20
HEAVY = pl.CostEstimate(flops=1 << 37, bytes_accessed=1 << 18, transcendentals=0)
LIGHT = pl.CostEstimate(flops=1 << 20, bytes_accessed=1 << 18, transcendentals=0)


def send(value, axis, by):
    count = lax.axis_size(axis)
    return lax.ppermute(value, axis, [(i, (i + by) % count) for i in range(count)])


def send_along_tokens(value, by):
    count = lax.axis_size("z") * lax.axis_size("x")
    pairs = [(i, i + by) for i in range(count) if 0 <= i + by < count]
    return lax.ppermute(value, ("z", "x"), pairs)


def after(value, *others):
    return lax.optimization_barrier((value, *others))[0]


def product(a, b):
    return (a.astype(F32) * b.astype(F32)).astype(BF16)


def anti_identity(size):
    at = sum(lax.broadcasted_iota(jnp.int32, (size, size), i) for i in range(2))
    return (at == size - 1).astype(F32).astype(BF16)


def group_tables(filters, reverse):
    taps = filters.shape[1]
    if reverse:
        filters = jnp.dot(filters, anti_identity(taps), preferred_element_type=F32)
    rows = jnp.concatenate([filters.astype(F32), jnp.zeros(filters.shape, F32)], 1)
    tables = [
        pltpu.roll(
            jnp.broadcast_to(rows[g : g + 1], (taps, 2 * taps)), int(reverse), 1, stride=1, stride_axis=0
        )
        for g in range(rows.shape[0])
    ]
    return jnp.concatenate(tables, 0).astype(BF16)


def banded(tables, window, taps, groups):
    lane_group = lax.broadcasted_iota(jnp.int32, (taps, LANES), 1) // (LANES // groups)
    blocks = window.shape[0] // taps - 1
    out = []
    for b in range(0, blocks, 2):
        pair = jnp.concatenate(
            [window[(b + i) * taps : (b + i + 2) * taps] for i in range(2)], 1
        )
        res = jnp.dot(tables, pair, preferred_element_type=F32)
        for i in range(2):
            cols = slice(i * LANES, (i + 1) * LANES)
            acc = res[:taps, cols]
            for g in range(1, groups):
                acc = jnp.where(lane_group == g, res[g * taps : (g + 1) * taps, cols], acc)
            out.append(acc)
    return jnp.concatenate(out, 0)


def forward_body(taps, groups, filters_ref, k_ref, v_ref, q_ref, rim_ref, *refs):
    conv_ref, mixed_ref, gated_ref = refs[-3:]
    mixed = product(k_ref[...], v_ref[...])
    window = jnp.concatenate([rim_ref[...], mixed], 0)
    conv = banded(group_tables(filters_ref[...], True), window, taps, groups)
    conv_ref[...] = conv
    mixed_ref[...] = mixed
    gated_ref[...] = (q_ref[...].astype(F32) * conv).astype(BF16)


def forward(half, filters, k, v, q, rim, earlier):
    tokens, width = k.shape
    taps = rim.shape[0]
    groups = LANES * filters.shape[0] // width
    steps = width // LANES // 2
    at = lambda i: (0, i + half * steps)
    column = pl.BlockSpec((tokens, LANES), at)
    in_specs = [
        pl.BlockSpec((groups, taps), lambda i: (i + half * steps, 0)),
        column,
        column,
        column,
        pl.BlockSpec((taps, LANES), at),
    ]
    args = [filters, k, v, q, rim]
    aliases = {}
    if earlier is not None:
        in_specs += [pl.BlockSpec(memory_space=pl.ANY)] * 2
        args += list(earlier)
        aliases = {5: 0, 6: 1}
    return pl.pallas_call(
        functools.partial(forward_body, taps, groups),
        grid=(steps,),
        in_specs=in_specs,
        out_specs=[column, column, pl.BlockSpec((tokens, LANES), lambda i: (0, i))],
        out_shape=[
            jax.ShapeDtypeStruct((tokens, width), F32),
            jax.ShapeDtypeStruct((tokens, width), BF16),
            jax.ShapeDtypeStruct((tokens, width // 2), BF16),
        ],
        input_output_aliases=aliases,
        compiler_params=pltpu.CompilerParams(vmem_limit_bytes=16 * MIB),
        cost_estimate=LIGHT,
        name="conv_forward",
    )(*args)


def join_body(*refs):
    pieces, out_ref = refs[:-2], refs[-1]
    rows = pieces[0].shape[0]
    for i, ref in enumerate(pieces):
        out_ref[i * rows : (i + 1) * rows] = ref[...]


def join(pieces, later_than):
    rows, width = pieces[0].shape
    return pl.pallas_call(
        join_body,
        in_specs=[pl.BlockSpec(memory_space=pltpu.VMEM)] * len(pieces) + [pl.BlockSpec(memory_space=pl.ANY)],
        out_specs=pl.BlockSpec(memory_space=pltpu.VMEM),
        out_shape=jax.ShapeDtypeStruct((len(pieces) * rows, width), pieces[0].dtype),
        compiler_params=pltpu.CompilerParams(vmem_limit_bytes=4 * MIB),
        cost_estimate=LIGHT,
        name="join",
    )(*pieces, later_than)


def gate_body(wanted, place_ref, mine_ref, sib_ref, proj_ref, *refs):
    added, outs = refs[:-2], refs[-2:]
    rows = proj_ref.shape[0] // 8
    tokens, half = outs[0].shape
    tile = 256
    for n, (block, side) in enumerate(wanted):
        at = pl.ds(block * tokens, tokens)
        lhs = [jnp.concatenate([mine_ref[dy, at], sib_ref[dy, at]], 1) for dy in range(4)]
        for start in range(0, half, tile):
            cols = pl.ds(side * half + start, tile)
            acc = None
            for dy in range(4):
                rhs = jnp.concatenate(
                    [
                        proj_ref[pl.ds(pl.multiple_of(place_ref[2 * dy + i] * rows, rows), rows), cols]
                        for i in range(2)
                    ],
                    0,
                )
                term = jnp.dot(lhs[dy], rhs, preferred_element_type=F32)
                acc = term if acc is None else acc + term
            here = pl.ds(start, tile)
            if added:
                acc = acc + added[n][:, here].astype(F32)
            outs[n][:, here] = acc.astype(outs[n].dtype)


RESIDENT = pl.BlockSpec(memory_space=pltpu.VMEM)


def gate_parts(place, mine, sib, proj, wanted, dtype, *added):
    width = proj.shape[1]
    tokens = mine.shape[1] // 4
    return pl.pallas_call(
        functools.partial(gate_body, wanted),
        in_specs=[pl.BlockSpec(memory_space=pltpu.SMEM)] + [RESIDENT] * (3 + len(added)),
        out_specs=[RESIDENT] * 2,
        out_shape=[jax.ShapeDtypeStruct((tokens, width // 2), dtype)] * 2,
        compiler_params=pltpu.CompilerParams(vmem_limit_bytes=14 * MIB),
        cost_estimate=LIGHT,
        name="grad_gate_parts",
    )(place, mine, sib, proj, *added)


def proj_body(place_ref, mine_ref, sib_ref, *refs):
    gated_refs, out_ref = refs[:-1], refs[-1]
    rows = mine_ref.shape[2]
    tokens, half = gated_refs[0].shape
    for dy in range(4):
        lhs = [
            jnp.concatenate([mine_ref[dy, at], sib_ref[dy, at]], 1)
            for at in (pl.ds(d * tokens, tokens) for d in range(4))
        ]
        for h in range(2):
            acc = None
            for d in range(4):
                term = lax.dot_general(
                    lhs[d],
                    gated_refs[2 * d + h][...],
                    (((0,), (0,)), ((), ())),
                    preferred_element_type=F32,
                )
                acc = term if acc is None else acc + term
            acc = acc.astype(BF16)
            cols = pl.ds(h * half, half)
            for i in range(2):
                to = pl.ds(pl.multiple_of(place_ref[2 * dy + i] * rows, rows), rows)
                out_ref[to, cols] = acc[i * rows : (i + 1) * rows]


def proj_part(place, mine, sib, gated):
    half = gated[0].shape[1]
    return pl.pallas_call(
        proj_body,
        in_specs=[pl.BlockSpec(memory_space=pltpu.SMEM)] + [RESIDENT] * 10,
        out_specs=RESIDENT,
        out_shape=jax.ShapeDtypeStruct((8 * mine.shape[2], 2 * half), BF16),
        compiler_params=pltpu.CompilerParams(vmem_limit_bytes=14 * MIB),
        cost_estimate=LIGHT,
        name="grad_proj_part",
    )(place, mine, sib, *gated)


def inner_body(*refs):
    own, from_left, from_right = refs[0:2], refs[2:4], refs[4:6]
    q_ref, conv_ref, query_ref, inner_ref, first_ref = refs[6:]
    step, half_steps, wide = pl.program_id(0), pl.num_programs(0) // 2, inner_ref.shape[1]
    here = pl.ds(pl.multiple_of(step % half_steps * wide, wide), wide)
    pick = lambda pair: jnp.where(step >= half_steps, pair[1][:, here], pair[0][:, here]).astype(F32)
    gate = pick(own) + pick(from_left) + pick(from_right)
    query_ref[...] = (gate * conv_ref[...]).astype(BF16)
    inner = (gate * q_ref[...].astype(F32)).astype(BF16)
    inner_ref[...] = inner
    first_ref[...] = inner[: first_ref.shape[0]]


def gate_gradients(own, from_left, from_right, q, conv, taps):
    tokens, width = q.shape
    wide = 2 * LANES
    steps = width // wide
    column = pl.BlockSpec((tokens, wide), lambda i: (0, i))
    return pl.pallas_call(
        inner_body,
        grid=(steps,),
        in_specs=[RESIDENT] * 6 + [column, column],
        out_specs=[column, column, pl.BlockSpec((taps, wide), lambda i: (0, i))],
        out_shape=[jax.ShapeDtypeStruct((n, width), BF16) for n in (tokens, tokens, taps)],
        compiler_params=pltpu.CompilerParams(vmem_limit_bytes=16 * MIB),
        cost_estimate=LIGHT,
        name="gate_gradients",
    )(*own, *from_left, *from_right, q, conv)


def filter_body(taps, groups, inner_ref, mixed_ref, rim_ref, filter_ref):
    inner = inner_ref[...]
    window = jnp.concatenate([rim_ref[...], mixed_ref[...]], 0)
    blocks = inner.shape[0] // taps
    left = jnp.concatenate([inner[b * taps : (b + 1) * taps] for b in range(blocks)], 1)
    left = jnp.dot(anti_identity(taps), left, preferred_element_type=F32).astype(BF16)
    right = jnp.concatenate([window[b * taps : (b + 2) * taps] for b in range(blocks)], 1)
    lane_group = (lax.broadcasted_iota(jnp.int32, left.shape, 1) % LANES) // (LANES // groups)
    zero = jnp.zeros_like(left)
    stacked = jnp.concatenate([jnp.where(lane_group == g, left, zero) for g in range(groups)], 0)
    corr = lax.dot_general(stacked, right, (((1,), (1,)), ((), ())), preferred_element_type=F32)
    sums = [
        jnp.sum(
            pltpu.roll(corr[g * taps : (g + 1) * taps], 0, 1, stride=1, stride_axis=0),
            axis=0,
            keepdims=True,
        )[:, taps:]
        for g in range(groups)
    ]
    filter_ref[...] = jnp.concatenate(sums, 0)


def filter_part(inner, mixed, rim, group_count):
    tokens, width = inner.shape
    taps = rim.shape[0]
    groups = LANES * group_count // width
    column = pl.BlockSpec((tokens, LANES), lambda i: (0, i))
    return pl.pallas_call(
        functools.partial(filter_body, taps, groups),
        grid=(width // LANES,),
        in_specs=[column, column, pl.BlockSpec((taps, LANES), lambda i: (0, i))],
        out_specs=pl.BlockSpec((groups, taps), lambda i: (i, 0)),
        out_shape=jax.ShapeDtypeStruct((group_count, taps), F32),
        compiler_params=pltpu.CompilerParams(vmem_limit_bytes=16 * MIB),
        cost_estimate=HEAVY,
        name="filter_part",
    )(inner, mixed, rim)


def backward_body(taps, groups, filters_ref, inner_ref, ahead_ref, k_ref, v_ref, *refs):
    gk_ref, gv_ref = refs[-2:]
    window = jnp.concatenate([inner_ref[...], ahead_ref[...]], 0)
    grad = banded(group_tables(filters_ref[...], False), window, taps, groups)
    gk_ref[...] = (grad * v_ref[...].astype(F32)).astype(BF16)
    gv_ref[...] = (grad * k_ref[...].astype(F32)).astype(BF16)


def backward(half, filters, inner, ahead, k, v, earlier):
    tokens, width = k.shape
    taps = ahead.shape[0]
    groups = LANES * filters.shape[0] // width
    steps = width // LANES // 2
    at = lambda i: (0, i + half * steps)
    column = pl.BlockSpec((tokens, LANES), at)
    in_specs = [
        pl.BlockSpec((groups, taps), lambda i: (i + half * steps, 0)),
        column,
        pl.BlockSpec((taps, LANES), at),
        column,
        column,
    ]
    args = [filters, inner, ahead, k, v]
    aliases = {}
    if earlier is not None:
        in_specs += [pl.BlockSpec(memory_space=pl.ANY)] * 2
        args += list(earlier)
        aliases = {5: 0, 6: 1}
    return pl.pallas_call(
        functools.partial(backward_body, taps, groups),
        grid=(steps,),
        in_specs=in_specs,
        out_specs=[column, column],
        out_shape=[jax.ShapeDtypeStruct((tokens, width), BF16)] * 2,
        input_output_aliases=aliases,
        compiler_params=pltpu.CompilerParams(vmem_limit_bytes=16 * MIB),
        cost_estimate=LIGHT,
        name="conv_backward",
    )(*args)


def sum_over(value, axis, stride, *beside):
    count, me = lax.axis_size(axis) // stride, lax.axis_index(axis) // stride
    terms = [after(value, *beside)] + [send(value, axis, d * stride) for d in range(1, count)]
    total = None
    for source in range(count):
        term = terms[0]
        for d in range(1, count):
            term = jnp.where((me - source) % count == d, terms[d], term)
        total = term if total is None else total + term
    return total


def on_device(query_in, key_in, value_in, filters, proj_out, cotangent):
    tokens, width = query_in.shape
    group_count, taps = filters.shape
    half = width // 2
    x, y, c = (lax.axis_index(a) for a in ("x", "y", "c"))
    part = cotangent.shape[1] // 4

    proj = lax.all_gather(proj_out, "z", axis=0, tiled=True)

    last = product(key_in[tokens - taps :], value_in[tokens - taps :])
    rim = send_along_tokens(last, 1)
    base = after(x, last)
    own_cols = lambda d: lax.dynamic_slice_in_dim(cotangent, ((base + d) % 4) * part, part, 1)
    pieces = [own_cols(0), None, None, None]
    for d in (2, 1, 3):
        pieces[(-d) % 4] = send(own_cols(d), "x", d)
    conv, mixed, gated_a = forward(0, filters, key_in, value_in, query_in, rim, None)
    conv, mixed, gated_b = forward(1, filters, key_in, value_in, query_in, rim, (conv, mixed))
    column = join(pieces, gated_b)
    below, above = send(column, "y", 1), send(column, "y", -1)
    middle = column.shape[0] // 2
    far = send(below[:middle], "y", 1), send(above[middle:], "y", -1)
    left_a, right_a = send(gated_a, "x", 1), send(gated_a, "x", -1)
    right_b, left_b = send(gated_b, "x", -1), send(after(gated_b, left_a), "x", 1)
    far_a, far_b = send(left_a, "x", 1), send(right_b, "x", -1)
    gated = [gated_a, gated_b, right_a, right_b, far_a, far_b, left_a, left_b]

    far = after(far[0], left_a, right_b), far[1]
    mine = jnp.concatenate([column, above, *far, below], 0).reshape(4, 4 * tokens, part)
    sib = send(after(mine, right_a, left_b), "c", 1)
    place = jnp.stack([2 * ((y + dy) % 4) + (c if i == 0 else 1 - c) for dy in range(4) for i in range(2)])
    place = place.astype(jnp.int32)

    across = gate_parts(place, mine, sib, proj, ((2, 0), (2, 1)), BF16)
    far_a, far_b = send(across[0], "x", 1), send(across[1], "x", -1)
    proj = after(proj, *across, *gated[4:6])
    beside = gate_parts(place, mine, sib, proj, ((1, 1), (3, 0)), BF16)
    from_left_b, from_right_a = send(beside[0], "x", 1), send(beside[1], "x", -1)
    gated[0] = after(gated[0], *beside)
    proj_sums = proj_part(place, mine, sib, gated)

    joined = gate_parts(place, mine, sib, proj, ((1, 0), (3, 1)), BF16, after(far_a, proj_sums), far_b)
    from_left_a, from_right_b = send(joined[0], "x", 1), send(joined[1], "x", -1)
    grad_proj = lax.psum_scatter(proj_sums, "z", scatter_dimension=0, tiled=True).astype(F32)
    own = gate_parts(place, mine, sib, proj, ((0, 0), (0, 1)), F32)
    from_left, from_right = (from_left_a, from_left_b), (from_right_a, from_right_b)

    grad_query, inner, first = gate_gradients(own, from_left, from_right, query_in, conv, taps)
    ahead = send_along_tokens(first, -1)
    sums = filter_part(inner, mixed, rim, group_count)
    grads = backward(0, filters, after(inner, sums), ahead, key_in, value_in, None)
    sums = sum_over(sums, "x", 1, *grads)
    grad_key, grad_value = backward(1, filters, after(inner, sums), ahead, key_in, value_in, grads)
    sums = sum_over(sums, "z", 2, grad_key)
    odd = lax.ppermute(sums, "z", [(i, i ^ 1) for i in range(lax.axis_size("z"))])
    grad_filter = jnp.flip(after(sums, grad_proj) + odd, 1)
    return grad_query, grad_key, grad_value, grad_filter, grad_proj


def solution(mesh):
    ctx, tp = mesh.devices.shape
    shape = (ctx // SIZE["x"], SIZE["x"], tp // SIZE["c"], SIZE["c"])
    fine = Mesh(mesh.devices.reshape(shape), AXES)
    spec, along = P(("z", "x"), ("y", "c")), P(("y", "c"), None)
    return jax.shard_map(
        on_device,
        mesh=fine,
        in_specs=(spec, spec, spec, along, spec, spec),
        out_specs=(spec, spec, spec, along, spec),
        check_vma=False,
    )
```

```python
import functools

import jax
import jax.numpy as jnp
from jax import lax
from jax.experimental import pallas as pl
from jax.experimental.pallas import tpu as pltpu
from jax.sharding import Mesh
from jax.sharding import PartitionSpec as P

F32, BF16 = jnp.float32, jnp.bfloat16
LANES = 128
AXES = ("z", "x", "y", "c")
SIZE = {"x": 4, "y": 4, "c": 2}
MIB = 1 << 20
HEAVY = pl.CostEstimate(flops=1 << 37, bytes_accessed=1 << 18, transcendentals=0)
LIGHT = pl.CostEstimate(flops=1 << 20, bytes_accessed=1 << 18, transcendentals=0)


def send(value, axis, by):
    count = lax.axis_size(axis)
    return lax.ppermute(value, axis, [(i, (i + by) % count) for i in range(count)])


def send_along_tokens(value, by):
    count = lax.axis_size("z") * lax.axis_size("x")
    pairs = [(i, i + by) for i in range(count) if 0 <= i + by < count]
    return lax.ppermute(value, ("z", "x"), pairs)


def after(value, *others):
    return lax.optimization_barrier((value, *others))[0]


def product(a, b):
    return (a.astype(F32) * b.astype(F32)).astype(BF16)


def anti_identity(size):
    at = sum(lax.broadcasted_iota(jnp.int32, (size, size), i) for i in range(2))
    return (at == size - 1).astype(F32).astype(BF16)


def group_tables(filters, reverse):
    taps = filters.shape[1]
    if reverse:
        filters = jnp.dot(filters.astype(BF16), anti_identity(taps), preferred_element_type=F32)
    rows = jnp.concatenate([filters, jnp.zeros(filters.shape, F32)], 1)
    tables = [
        pltpu.roll(
            jnp.broadcast_to(rows[g : g + 1], (taps, 2 * taps)), int(reverse), 1, stride=1, stride_axis=0
        )
        for g in range(rows.shape[0])
    ]
    return jnp.concatenate(tables, 0).astype(BF16)


def banded(tables, window, taps, groups):
    lane_group = lax.broadcasted_iota(jnp.int32, (taps, LANES), 1) // (LANES // groups)
    blocks = window.shape[0] // taps - 1
    out = []
    for b in range(0, blocks, 2):
        pair = jnp.concatenate(
            [window[(b + i) * taps : (b + i + 2) * taps] for i in range(2)], 1
        )
        res = jnp.dot(tables, pair, preferred_element_type=F32)
        for i in range(2):
            cols = slice(i * LANES, (i + 1) * LANES)
            acc = res[:taps, cols]
            for g in range(1, groups):
                acc = jnp.where(lane_group == g, res[g * taps : (g + 1) * taps, cols], acc)
            out.append(acc)
    return jnp.concatenate(out, 0)


def forward_body(taps, groups, filters_ref, k_ref, v_ref, q_ref, rim_ref, *refs):
    conv_ref, mixed_ref, gated_ref = refs[-3:]
    mixed = product(k_ref[...], v_ref[...])
    window = jnp.concatenate([rim_ref[...], mixed], 0)
    conv = banded(group_tables(filters_ref[...], True), window, taps, groups)
    conv_ref[...] = conv
    mixed_ref[...] = mixed
    gated_ref[...] = (q_ref[...].astype(F32) * conv).astype(BF16)


def forward(half, filters, k, v, q, rim, earlier):
    tokens, width = k.shape
    taps = rim.shape[0]
    groups = LANES * filters.shape[0] // width
    steps = width // LANES // 2
    at = lambda i: (0, i + half * steps)
    column = pl.BlockSpec((tokens, LANES), at)
    in_specs = [
        pl.BlockSpec((groups, taps), lambda i: (i + half * steps, 0)),
        column,
        column,
        column,
        pl.BlockSpec((taps, LANES), at),
    ]
    args = [filters, k, v, q, rim]
    aliases = {}
    if earlier is not None:
        in_specs += [pl.BlockSpec(memory_space=pl.ANY)] * 2
        args += list(earlier)
        aliases = {5: 0, 6: 1}
    return pl.pallas_call(
        functools.partial(forward_body, taps, groups),
        grid=(steps,),
        in_specs=in_specs,
        out_specs=[column, column, pl.BlockSpec((tokens, LANES), lambda i: (0, i))],
        out_shape=[
            jax.ShapeDtypeStruct((tokens, width), F32),
            jax.ShapeDtypeStruct((tokens, width), BF16),
            jax.ShapeDtypeStruct((tokens, width // 2), BF16),
        ],
        input_output_aliases=aliases,
        compiler_params=pltpu.CompilerParams(vmem_limit_bytes=16 * MIB),
        cost_estimate=LIGHT,
        name="conv_forward",
    )(*args)


def join_body(*refs):
    pieces, out_ref = refs[:-2], refs[-1]
    rows = pieces[0].shape[0]
    for i, ref in enumerate(pieces):
        out_ref[i * rows : (i + 1) * rows] = ref[...]


def join(pieces, later_than):
    rows, width = pieces[0].shape
    return pl.pallas_call(
        join_body,
        in_specs=[pl.BlockSpec(memory_space=pltpu.VMEM)] * len(pieces) + [pl.BlockSpec(memory_space=pl.ANY)],
        out_specs=pl.BlockSpec(memory_space=pltpu.VMEM),
        out_shape=jax.ShapeDtypeStruct((len(pieces) * rows, width), pieces[0].dtype),
        compiler_params=pltpu.CompilerParams(vmem_limit_bytes=4 * MIB),
        cost_estimate=LIGHT,
        name="join",
    )(*pieces, later_than)


def gate_body(wanted, place_ref, mine_ref, sib_ref, proj_ref, *refs):
    added, outs = refs[:-2], refs[-2:]
    rows = proj_ref.shape[0] // 8
    tokens, half = outs[0].shape
    tile = 256
    for n, (block, side) in enumerate(wanted):
        at = pl.ds(block * tokens, tokens)
        lhs = [jnp.concatenate([mine_ref[dy, at], sib_ref[dy, at]], 1) for dy in range(4)]
        for start in range(0, half, tile):
            cols = pl.ds(side * half + start, tile)
            acc = None
            for dy in range(4):
                rhs = jnp.concatenate(
                    [
                        proj_ref[pl.ds(pl.multiple_of(place_ref[2 * dy + i] * rows, rows), rows), cols]
                        for i in range(2)
                    ],
                    0,
                )
                term = jnp.dot(lhs[dy], rhs, preferred_element_type=F32)
                acc = term if acc is None else acc + term
            here = pl.ds(start, tile)
            if added:
                acc = acc + added[n][:, here].astype(F32)
            outs[n][:, here] = acc.astype(outs[n].dtype)


RESIDENT = pl.BlockSpec(memory_space=pltpu.VMEM)


def gate_parts(place, mine, sib, proj, wanted, dtype, *added):
    width = proj.shape[1]
    tokens = mine.shape[1] // 4
    return pl.pallas_call(
        functools.partial(gate_body, wanted),
        in_specs=[pl.BlockSpec(memory_space=pltpu.SMEM)] + [RESIDENT] * (3 + len(added)),
        out_specs=[RESIDENT] * 2,
        out_shape=[jax.ShapeDtypeStruct((tokens, width // 2), dtype)] * 2,
        compiler_params=pltpu.CompilerParams(vmem_limit_bytes=14 * MIB),
        cost_estimate=LIGHT,
        name="grad_gate_parts",
    )(place, mine, sib, proj, *added)


def proj_body(place_ref, mine_ref, sib_ref, *refs):
    gated_refs, out_ref = refs[:-1], refs[-1]
    rows = mine_ref.shape[2]
    tokens, half = gated_refs[0].shape
    for dy in range(4):
        lhs = [
            jnp.concatenate([mine_ref[dy, at], sib_ref[dy, at]], 1)
            for at in (pl.ds(d * tokens, tokens) for d in range(4))
        ]
        for h in range(2):
            acc = None
            for d in range(4):
                term = lax.dot_general(
                    lhs[d],
                    gated_refs[2 * d + h][...],
                    (((0,), (0,)), ((), ())),
                    preferred_element_type=F32,
                )
                acc = term if acc is None else acc + term
            acc = acc.astype(BF16)
            cols = pl.ds(h * half, half)
            for i in range(2):
                to = pl.ds(pl.multiple_of(place_ref[2 * dy + i] * rows, rows), rows)
                out_ref[to, cols] = acc[i * rows : (i + 1) * rows]


def proj_part(place, mine, sib, gated):
    half = gated[0].shape[1]
    return pl.pallas_call(
        proj_body,
        in_specs=[pl.BlockSpec(memory_space=pltpu.SMEM)] + [RESIDENT] * 10,
        out_specs=RESIDENT,
        out_shape=jax.ShapeDtypeStruct((8 * mine.shape[2], 2 * half), BF16),
        compiler_params=pltpu.CompilerParams(vmem_limit_bytes=14 * MIB),
        cost_estimate=LIGHT,
        name="grad_proj_part",
    )(place, mine, sib, *gated)


def inner_body(*refs):
    own, from_left, from_right = refs[0:2], refs[2:4], refs[4:6]
    q_ref, conv_ref, query_ref, inner_ref, first_ref = refs[6:]
    step, half_steps, wide = pl.program_id(0), pl.num_programs(0) // 2, inner_ref.shape[1]
    here = pl.ds(pl.multiple_of(step % half_steps * wide, wide), wide)
    pick = lambda pair: jnp.where(step >= half_steps, pair[1][:, here], pair[0][:, here]).astype(F32)
    gate = pick(own) + pick(from_left) + pick(from_right)
    query_ref[...] = (gate * conv_ref[...]).astype(BF16)
    inner = (gate * q_ref[...].astype(F32)).astype(BF16)
    inner_ref[...] = inner
    first_ref[...] = inner[: first_ref.shape[0]]


def gate_gradients(own, from_left, from_right, q, conv, taps):
    tokens, width = q.shape
    wide = 2 * LANES
    steps = width // wide
    column = pl.BlockSpec((tokens, wide), lambda i: (0, i))
    return pl.pallas_call(
        inner_body,
        grid=(steps,),
        in_specs=[RESIDENT] * 6 + [column, column],
        out_specs=[column, column, pl.BlockSpec((taps, wide), lambda i: (0, i))],
        out_shape=[jax.ShapeDtypeStruct((n, width), BF16) for n in (tokens, tokens, taps)],
        compiler_params=pltpu.CompilerParams(vmem_limit_bytes=60 * MIB),
        cost_estimate=LIGHT,
        name="gate_gradients",
    )(*own, *from_left, *from_right, q, conv)


def filter_body(taps, groups, inner_ref, mixed_ref, rim_ref, filter_ref):
    inner = inner_ref[...]
    window = jnp.concatenate([rim_ref[...], mixed_ref[...]], 0)
    blocks = inner.shape[0] // taps
    left = jnp.concatenate([inner[b * taps : (b + 1) * taps] for b in range(blocks)], 1)
    left = jnp.dot(anti_identity(taps), left, preferred_element_type=F32).astype(BF16)
    right = jnp.concatenate([window[b * taps : (b + 2) * taps] for b in range(blocks)], 1)
    lane_group = (lax.broadcasted_iota(jnp.int32, left.shape, 1) % LANES) // (LANES // groups)
    zero = jnp.zeros_like(left)
    stacked = jnp.concatenate([jnp.where(lane_group == g, left, zero) for g in range(groups)], 0)
    corr = lax.dot_general(stacked, right, (((1,), (1,)), ((), ())), preferred_element_type=F32)
    sums = [
        jnp.sum(
            pltpu.roll(corr[g * taps : (g + 1) * taps], 0, 1, stride=1, stride_axis=0),
            axis=0,
            keepdims=True,
        )[:, taps:]
        for g in range(groups)
    ]
    filter_ref[...] = jnp.concatenate(sums, 0)


def filter_part(inner, mixed, rim, group_count):
    tokens, width = inner.shape
    taps = rim.shape[0]
    groups = LANES * group_count // width
    column = pl.BlockSpec((tokens, LANES), lambda i: (0, i))
    return pl.pallas_call(
        functools.partial(filter_body, taps, groups),
        grid=(width // LANES,),
        in_specs=[column, column, pl.BlockSpec((taps, LANES), lambda i: (0, i))],
        out_specs=pl.BlockSpec((groups, taps), lambda i: (i, 0)),
        out_shape=jax.ShapeDtypeStruct((group_count, taps), F32),
        compiler_params=pltpu.CompilerParams(vmem_limit_bytes=60 * MIB),
        cost_estimate=HEAVY,
        name="filter_part",
    )(inner, mixed, rim)


def backward_body(taps, groups, filters_ref, inner_ref, ahead_ref, k_ref, v_ref, *refs):
    gk_ref, gv_ref = refs[-2:]
    window = jnp.concatenate([inner_ref[...], ahead_ref[...]], 0)
    grad = banded(group_tables(filters_ref[...], False), window, taps, groups)
    gk_ref[...] = (grad * v_ref[...].astype(F32)).astype(BF16)
    gv_ref[...] = (grad * k_ref[...].astype(F32)).astype(BF16)


def backward(half, filters, inner, ahead, k, v, earlier):
    tokens, width = k.shape
    taps = ahead.shape[0]
    groups = LANES * filters.shape[0] // width
    steps = width // LANES // 2
    at = lambda i: (0, i + half * steps)
    column = pl.BlockSpec((tokens, LANES), at)
    in_specs = [
        pl.BlockSpec((groups, taps), lambda i: (i + half * steps, 0)),
        column,
        pl.BlockSpec((taps, LANES), at),
        column,
        column,
    ]
    args = [filters, inner, ahead, k, v]
    aliases = {}
    if earlier is not None:
        in_specs += [pl.BlockSpec(memory_space=pl.ANY)] * 2
        args += list(earlier)
        aliases = {5: 0, 6: 1}
    return pl.pallas_call(
        functools.partial(backward_body, taps, groups),
        grid=(steps,),
        in_specs=in_specs,
        out_specs=[column, column],
        out_shape=[jax.ShapeDtypeStruct((tokens, width), BF16)] * 2,
        input_output_aliases=aliases,
        compiler_params=pltpu.CompilerParams(vmem_limit_bytes=16 * MIB),
        cost_estimate=LIGHT,
        name="conv_backward",
    )(*args)


def sum_over(value, axis, stride, *beside):
    count, me = lax.axis_size(axis) // stride, lax.axis_index(axis) // stride
    terms = [after(value, *beside)] + [send(value, axis, d * stride) for d in range(1, count)]
    total = None
    for source in range(count):
        term = terms[0]
        for d in range(1, count):
            term = jnp.where((me - source) % count == d, terms[d], term)
        total = term if total is None else total + term
    return total


def on_device(query_in, key_in, value_in, filters, proj_out, cotangent):
    tokens, width = query_in.shape
    group_count, taps = filters.shape
    half = width // 2
    x, y, c = (lax.axis_index(a) for a in ("x", "y", "c"))
    part = cotangent.shape[1] // 4
    filters = filters.astype(F32)

    proj = lax.all_gather(proj_out, "z", axis=0, tiled=True)

    last = product(key_in[tokens - taps :], value_in[tokens - taps :])
    rim = send_along_tokens(last, 1)
    base = after(x, last)
    own_cols = lambda d: lax.dynamic_slice_in_dim(cotangent, ((base + d) % 4) * part, part, 1)
    pieces = [own_cols(0), None, None, None]
    for d in (2, 1, 3):
        pieces[(-d) % 4] = send(own_cols(d), "x", d)
    conv, mixed, gated_a = forward(0, filters, key_in, value_in, query_in, rim, None)
    conv, mixed, gated_b = forward(1, filters, key_in, value_in, query_in, rim, (conv, mixed))
    column = join(pieces, gated_b)
    below, above = send(column, "y", 1), send(column, "y", -1)
    middle = column.shape[0] // 2
    far = send(below[:middle], "y", 1), send(above[middle:], "y", -1)
    left_a, right_a = send(gated_a, "x", 1), send(gated_a, "x", -1)
    right_b, left_b = send(gated_b, "x", -1), send(after(gated_b, left_a), "x", 1)
    far_a, far_b = send(left_a, "x", 1), send(right_b, "x", -1)
    gated = [gated_a, gated_b, right_a, right_b, far_a, far_b, left_a, left_b]

    far = after(far[0], left_a, right_b), far[1]
    mine = jnp.concatenate([column, above, *far, below], 0).reshape(4, 4 * tokens, part)
    sib = send(after(mine, right_a, left_b), "c", 1)
    place = jnp.stack([2 * ((y + dy) % 4) + (c if i == 0 else 1 - c) for dy in range(4) for i in range(2)])
    place = place.astype(jnp.int32)

    across = gate_parts(place, mine, sib, proj, ((2, 0), (2, 1)), BF16)
    far_a, far_b = send(across[0], "x", 1), send(across[1], "x", -1)
    proj = after(proj, *across, *gated[4:6])
    beside = gate_parts(place, mine, sib, proj, ((1, 1), (3, 0)), BF16)
    from_left_b, from_right_a = send(beside[0], "x", 1), send(beside[1], "x", -1)
    gated[0] = after(gated[0], *beside)
    proj_sums = proj_part(place, mine, sib, gated)

    joined = gate_parts(place, mine, sib, proj, ((1, 0), (3, 1)), BF16, after(far_a, proj_sums), far_b)
    from_left_a, from_right_b = send(joined[0], "x", 1), send(joined[1], "x", -1)
    grad_proj = lax.psum_scatter(proj_sums, "z", scatter_dimension=0, tiled=True).astype(F32)
    own = gate_parts(place, mine, sib, proj, ((0, 0), (0, 1)), F32)
    from_left, from_right = (from_left_a, from_left_b), (from_right_a, from_right_b)

    grad_query, inner, first = gate_gradients(own, from_left, from_right, query_in, conv, taps)
    ahead = send_along_tokens(first, -1)
    sums = filter_part(inner, mixed, rim, group_count)
    grads = backward(0, filters, after(inner, sums), ahead, key_in, value_in, None)
    sums = sum_over(sums, "x", 1, *grads)
    grad_key, grad_value = backward(1, filters, after(inner, sums), ahead, key_in, value_in, grads)
    sums = sum_over(sums, "z", 2, grad_key)
    odd = lax.ppermute(sums, "z", [(i, i ^ 1) for i in range(lax.axis_size("z"))])
    grad_filter = jnp.flip(after(sums, grad_proj) + odd, 1)
    return grad_query, grad_key, grad_value, grad_filter, grad_proj


def solution(mesh):
    ctx, tp = mesh.devices.shape
    shape = (ctx // SIZE["x"], SIZE["x"], tp // SIZE["c"], SIZE["c"])
    fine = Mesh(mesh.devices.reshape(shape), AXES)
    spec, along = P(("z", "x"), ("y", "c")), P(("y", "c"), None)
    return jax.shard_map(
        on_device,
        mesh=fine,
        in_specs=(spec, spec, spec, along, spec, spec),
        out_specs=(spec, spec, spec, along, spec),
        check_vma=False,
    )
```
